256 devices in a mesh: slab: 32 (over y_hi, z, core), blk: 8 (over x, y_lo).
Axes of the slice: x: 4, y: 4 (y_hi: 2, y_lo: 2; y = y_hi * 2 + y_lo), z: 8, core: 2. Of those that a mesh axis runs over, the one named last changes fastest.
Arguments:
- current: bfloat16 [768, 3, 96, 9, 128], P('blk', None, 'slab'), may hold values from -6 to 6
- search: bfloat16 [768, 3, 96, 9, 128], P('blk', None, 'slab'), may hold values from -6 to 6
- previous: bfloat16 [768, 3, 96, 9, 128], P('blk', None, 'slab'), may hold values from -6 to 6
- coefficients: bfloat16 [2304, 768], P('slab', 'blk'), may hold values from -0.125 to 0.125
- material: int32 [96, 9, 128], P('slab'), may hold values from 0 to 3
- inverse_permittivity: float32 [4, 3, 3], replicated, may hold values from -0.25 to 1, as said below
Outputs:
- applied: bfloat16 [768, 3, 96, 9, 128], P('blk', None, 'slab')
- rotated: bfloat16 [768, 3, 96, 9, 128], P('blk', None, 'slab')
- direction: bfloat16 [768, 3, 96, 9, 128], P('blk', None, 'slab')
The draws below stay inside these ranges and needn't reach their ends.
Inputs may be any that keep to these rules, and one draw needn't show every extreme that they name: `inverse_permittivity`: each material's tensor is symmetric; its diagonal entries lie in 0.08 to 1 and each entry off the diagonal is at most a quarter of the geometric mean of the two diagonal entries of its row and column.
All inputs are finite; a program needn't handle non-finite values.
Results may differ from the reference program's by a relative error of at most 0.003.
Values may be sent and summed in bfloat16 or wider, within the bound.
No kernel may reach another device: no remote copies, remote signals or barrier semaphores. Data moves between devices by JAX's collectives and lax.ppermute only.
A program may use at most 256 MiB of HBM per device.

```python
import jax
import jax.numpy as jnp
from jax import lax

M = 768
NMAT = 4
NX = 128
NY = 9
NZ = 96


def draw_inverse_permittivity(key, part):
    first_key, second_key = jax.random.split(jax.random.fold_in(key, 17))
    log_diag = jax.random.uniform(first_key, (NMAT, 3), jnp.float32, jnp.log(0.08), 0.0)
    diagonal = jnp.exp(log_diag)
    uniform = jax.random.uniform(second_key, (NMAT, 3, 3), jnp.float32, -0.25, 0.25)
    symmetric = 0.5 * (uniform + jnp.transpose(uniform, (0, 2, 1)))
    root = jnp.sqrt(diagonal)
    off_diag = symmetric * root[:, :, None] * root[:, None, :]
    identity = jnp.eye(3, dtype=jnp.float32)
    return identity[None] * diagonal[:, :, None] + (1.0 - identity[None]) * off_diag


def plant(values, stream_key, low, largest):
    place = [jax.random.randint(jax.random.fold_in(stream_key, axis), (), 0, length) for axis, length in enumerate(values.shape)]
    longest = values.shape.index(max(values.shape))
    beside = place[:longest] + [(place[longest] + 1) % values.shape[longest]] + place[longest + 1:]
    return values.at[tuple(place)].set(low).at[tuple(beside)].set(largest)


def steps_of(stream_key, shape, pieces, low, top_value):
    gain, own = 1.0, jax.random.fold_in(stream_key, 6)
    for position, blocks in pieces:
        draws = jnp.exp(jax.random.uniform(jax.random.fold_in(own, position), (blocks,), jnp.float32, low / len(pieces), top_value / len(pieces)))
        gain = gain * jnp.repeat(draws, shape[position] // blocks).reshape([-1 if axis == position else 1 for axis in range(len(shape))])
    return gain


def scatter_about(key, shape, scale, reach, shards=(), kind=jnp.bfloat16):
    drawn = jax.random.normal(key, shape, jnp.float32) * scale
    if len(shards) > 0:
        drawn = steps_of(key, shape, shards, -0.22, 0.18) * drawn
    return jnp.clip(drawn, min=-reach, max=reach).astype(kind)


def setup_inputs(seed: int = 0) -> dict:
    seeds = jax.random.split(jax.random.key(seed), 7)
    return {
        "current": scatter_about(seeds[0], (M, 3, NZ, NY, NX), 1.0, 6.0, ((0, 8), (2, 32))),
        "search": scatter_about(seeds[1], (M, 3, NZ, NY, NX), 1.0, 6.0, ((0, 8), (2, 32))),
        "previous": scatter_about(seeds[2], (M, 3, NZ, NY, NX), 1.0, 6.0, ((0, 8), (2, 32))),
        "coefficients": scatter_about(seeds[3], (3 * M, M), (3 * M) ** -0.5, 0.125, ((0, 32), (1, 8))),
        "material": plant(jax.random.randint(seeds[4], (NZ, NY, NX), 0, NMAT), jax.random.fold_in(seeds[4], 1), 0, NMAT - 1).astype(jnp.int32),
        "inverse_permittivity": draw_inverse_permittivity(jax.random.fold_in(seeds[6], 71), 0),
    }


def combine_curl(along_x, along_y, along_z):
    curl_x = along_y[:, 2] - along_z[:, 1]
    curl_y = along_z[:, 0] - along_x[:, 2]
    curl_z = along_x[:, 1] - along_y[:, 0]
    return curl_x, curl_y, curl_z


def forward_curl(field, tensor):
    centre = field[:, :, :-1]
    along_z = 0.5 * (field[:, :, 1:] - centre)
    along_y = 0.5 * (jnp.roll(centre, -1, axis=3) - centre)
    along_x = 0.5 * (jnp.roll(centre, -1, axis=4) - centre)
    curl_x, curl_y, curl_z = combine_curl(along_x, along_y, along_z)
    stacked = [tensor[which, 0] * curl_x + tensor[which, 1] * curl_y + tensor[which, 2] * curl_z for which in range(3)]
    return jnp.stack(stacked, axis=1)


def backward_curl(field):
    centre = field[:, :, 1:]
    along_z = 0.5 * (centre - field[:, :, :-1])
    along_y = 0.5 * (centre - jnp.roll(centre, 1, axis=3))
    along_x = 0.5 * (centre - jnp.roll(centre, 1, axis=4))
    curl_x, curl_y, curl_z = combine_curl(along_x, along_y, along_z)
    return jnp.stack([curl_x, curl_y, curl_z], axis=1)


def reference(current, search, previous, coefficients, material, inverse_permittivity):
    tensor = jnp.moveaxis(inverse_permittivity[material], (3, 4), (0, 1))

    def apply_group(group):
        field = group.astype(jnp.float32)
        extended = jnp.concatenate([field, field[:, :, :1]], axis=2)
        electric = forward_curl(extended, tensor)
        padded = jnp.concatenate([electric[:, :, -1:], electric], axis=2)
        return backward_curl(padded).astype(jnp.bfloat16)

    groups = search.reshape((8, M // 8) + search.shape[1:])
    applied = lax.map(apply_group, groups).reshape(search.shape)

    coef_current = coefficients[:M]
    coef_search = coefficients[M:2 * M]
    coef_previous = coefficients[2 * M:]

    def rotate(coef, block):
        return jnp.dot(coef.T, block, preferred_element_type=jnp.float32)

    rotated_parts = []
    direction_parts = []
    for which in range(3):
        direction_sum = rotate(coef_search, search[:, which].reshape(M, -1)) + rotate(coef_previous, previous[:, which].reshape(M, -1))
        rotated_sum = rotate(coef_current, current[:, which].reshape(M, -1)) + direction_sum
        direction_parts.append(direction_sum.astype(jnp.bfloat16).reshape(M, NZ, NY, NX))
        rotated_parts.append(rotated_sum.astype(jnp.bfloat16).reshape(M, NZ, NY, NX))
    rotated = jnp.stack(rotated_parts, axis=1)
    direction = jnp.stack(direction_parts, axis=1)
    return applied, rotated, direction
```

```python
import functools
import itertools

import jax
import jax.numpy as jnp
from jax import lax
from jax.experimental import pallas as pl
from jax.experimental.pallas import tpu as pltpu
from jax.sharding import PartitionSpec as P

M = 768
NMAT = 4
V = 96
NB = 8
ROWS = 81
SHARE = 10
LANES = 128 // NB
SLAB = (2, 8, 2)
BLK = (4, 2)
ANY = pl.BlockSpec(memory_space=pl.ANY)
VMEM_LIMIT = 56 * 1024 * 1024


def move(x, axis, sizes, steps):
    pairs = []
    for place in itertools.product(*[range(n) for n in sizes]):
        src = dst = 0
        for n, p, s in zip(sizes, place, steps):
            src = src * n + p
            dst = dst * n + (p + s) % n
        pairs.append((src, dst))
    return lax.ppermute(x, axis, pairs)


def ring_shift(x, axis, by):
    count = lax.axis_size(axis)
    return lax.ppermute(x, axis, [(i, (i + by) % count) for i in range(count)])


def in_order(parts, me):
    count = len(parts)
    if count == 2:
        first = jnp.where(me == 0, parts[0], parts[1])
        second = jnp.where(me == 0, parts[1], parts[0])
        return jnp.stack([first, second])
    twice = jnp.stack(parts + parts)
    return lax.dynamic_slice_in_dim(twice, (count - me) % count, count, 0)


def gather_coefficients(tile):
    slab, blk = lax.axis_index("slab"), lax.axis_index("blk")
    y_hi, z, core = slab // 16, (slab // 2) % 8, slab % 2
    x, y_lo = blk // 2, blk % 2
    t = in_order([tile, move(tile, "blk", BLK, (0, 1))], y_lo)
    t = in_order([t] + [move(t, "blk", BLK, (-k, 0)) for k in (1, 2, 3)], x)
    t = in_order([t, move(t, "slab", SLAB, (1, 0, 0))], y_hi)
    got = {0: t}
    for k in (1, 2, 3, 4):
        got[k] = move(got[k - 1], "slab", SLAB, (0, -1, 0))
        if k < 4:
            got[-k] = move(got[1 - k], "slab", SLAB, (0, 1, 0))
    t = in_order([got[k if k <= 4 else k - 8] for k in range(8)], z)
    t = in_order([t, move(t, "slab", SLAB, (0, 0, 1))], core)
    return t.transpose(3, 4, 6, 2, 1, 0, 5).reshape(M, 3 * M)


def lane_index(shape):
    return lax.broadcasted_iota(jnp.int32, shape, len(shape) - 1)


def rolled(x, by):
    by %= 128
    return x if by == 0 else pltpu.roll(x, by, x.ndim - 1)


def pack_kernel(w_ref, p_ref, x_ref, out_ref, tail, mixed, sems, tail_sems, out_sems):
    fields = (w_ref, p_ref, x_ref)
    copies = []
    for d in range(NB):
        for k, ref in enumerate(fields):
            copies.append(
                pltpu.make_async_copy(
                    ref.at[pl.ds(SHARE * d, SHARE)],
                    out_ref.at[d, pl.ds(SHARE * k, SHARE)],
                    sems.at[3 * d + k],
                )
            )
    last = [
        pltpu.make_async_copy(ref.at[ROWS - 1], tail.at[k], tail_sems.at[k])
        for k, ref in enumerate(fields)
    ]
    for c in last + copies:
        c.start()
    for c in last:
        c.wait()
    lane = lane_index((V, 128))
    w, p, x = (tail[k].astype(jnp.float32) for k in range(3))
    sends = []
    for d in range(NB):
        row = jnp.where(lane < 3 * LANES, rolled(x, LANES * (2 - d)), 0.0)
        row = jnp.where(lane < 2 * LANES, rolled(p, LANES * (1 - d)), row)
        row = jnp.where(lane < LANES, rolled(w, LANES * (0 - d)), row)
        mixed[d] = row.astype(jnp.bfloat16)
        sends.append(
            pltpu.make_async_copy(mixed.at[d], out_ref.at[d, 3 * SHARE], out_sems.at[d])
        )
        sends[-1].start()
    for c in copies + sends:
        c.wait()


def pack(w, p, x):
    return pl.pallas_call(
        pack_kernel,
        out_shape=jax.ShapeDtypeStruct((NB, 3 * SHARE + 1, V, 128), jnp.bfloat16),
        in_specs=[ANY] * 3,
        out_specs=ANY,
        scratch_shapes=[
            pltpu.VMEM((3, V, 128), jnp.bfloat16),
            pltpu.VMEM((NB, V, 128), jnp.bfloat16),
            pltpu.SemaphoreType.DMA((3 * NB,)),
            pltpu.SemaphoreType.DMA((3,)),
            pltpu.SemaphoreType.DMA((NB,)),
        ],
        compiler_params=pltpu.CompilerParams(vmem_limit_bytes=VMEM_LIMIT),
        name="pack",
    )(w, p, x)


def rotate_kernel(cells_ref, coef_ref, out_ref, cells, out, in_sems, out_sems):
    def fetch(k, i):
        rows = pl.ds(SHARE * k + 2 * i, 2)
        return pltpu.make_async_copy(
            cells_ref.at[:, rows], cells.at[:, rows], in_sems.at[k, i]
        )

    def put(k, i):
        rows = pl.ds(SHARE * k + 2 * i, 2)
        return pltpu.make_async_copy(
            out.at[:, rows], out_ref.at[:, rows], out_sems.at[k, i]
        )

    steps = SHARE // 2
    fetch_tail = pltpu.make_async_copy(
        cells_ref.at[:, pl.ds(3 * SHARE, 1)],
        cells.at[:, pl.ds(3 * SHARE, 1)],
        in_sems.at[0, steps],
    )
    put_tail = pltpu.make_async_copy(
        out.at[:, pl.ds(2 * SHARE, 1)],
        out_ref.at[:, pl.ds(2 * SHARE, 1)],
        out_sems.at[0, steps],
    )
    for i in range(steps):
        for k in range(3):
            fetch(k, i).start()
    fetch_tail.start()

    def product(w, p, x):
        wp = jnp.concatenate([w, p], axis=0)
        direction = jnp.dot(
            coef_ref[:, M:], wp, preferred_element_type=jnp.float32
        )
        rotated = direction + jnp.dot(
            coef_ref[:, :M], x, preferred_element_type=jnp.float32
        )
        return direction, rotated

    def step(i, carry):
        for k in range(3):
            fetch(k, i).wait()

        def row_pair(k):
            first = cells[:, SHARE * k + 2 * i].reshape(M, 128)
            second = cells[:, SHARE * k + 2 * i + 1].reshape(M, 128)
            return jnp.concatenate([first, second], axis=1)

        results = product(row_pair(0), row_pair(1), row_pair(2))
        for k, result in enumerate(results):
            result = result.astype(jnp.bfloat16)
            for j in range(2):
                part = result[:, 128 * j : 128 * (j + 1)]
                out[:, SHARE * k + 2 * i + j] = part.reshape(NB, V, 128)
            put(k, i).start()
        return carry

    lax.fori_loop(0, steps, step, 0)
    fetch_tail.wait()
    tail = cells[:, 3 * SHARE].reshape(M, 128)
    wide = tail.astype(jnp.float32)
    shifted = [rolled(wide, -LANES * k).astype(jnp.bfloat16) for k in (1, 2)]
    direction, rotated = product(tail, *shifted)
    mixed = jnp.where(
        lane_index((M, 128)) < LANES, direction, rolled(rotated, LANES)
    )
    out[:, 2 * SHARE] = mixed.astype(jnp.bfloat16).reshape(NB, V, 128)
    put_tail.start()
    for k in range(2):
        for i in range(steps):
            put(k, i).wait()
    put_tail.wait()


def rotate(cells, coef):
    return pl.pallas_call(
        rotate_kernel,
        out_shape=jax.ShapeDtypeStruct((NB, 2 * SHARE + 1, V, 128), jnp.bfloat16),
        in_specs=[ANY, pl.BlockSpec(memory_space=pltpu.VMEM)],
        out_specs=ANY,
        scratch_shapes=[
            pltpu.VMEM((NB, 3 * SHARE + 1, V, 128), jnp.bfloat16),
            pltpu.VMEM((NB, 2 * SHARE + 1, V, 128), jnp.bfloat16),
            pltpu.SemaphoreType.DMA((3, SHARE // 2 + 1)),
            pltpu.SemaphoreType.DMA((2, SHARE // 2 + 1)),
        ],
        compiler_params=pltpu.CompilerParams(vmem_limit_bytes=VMEM_LIMIT),
        cost_estimate=pl.CostEstimate(
            flops=6 * M * M * 128 * (SHARE + 1), bytes_accessed=14_000_000, transcendentals=0
        ),
        name="rotate",
    )(cells, coef)


def unpack_kernel(in_ref, d_ref, r_ref, tail, last, sems, tail_sems, last_sems):
    copies = []
    for s in range(NB):
        for k, ref in enumerate((d_ref, r_ref)):
            copies.append(
                pltpu.make_async_copy(
                    in_ref.at[s, pl.ds(SHARE * k, SHARE)],
                    ref.at[pl.ds(SHARE * s, SHARE)],
                    sems.at[2 * s + k],
                )
            )
    tails = [
        pltpu.make_async_copy(in_ref.at[s, 2 * SHARE], tail.at[s], tail_sems.at[s])
        for s in range(NB)
    ]
    for c in tails + copies:
        c.start()
    for c in tails:
        c.wait()
    which = lane_index((V, 128)) // LANES
    direction = rotated = jnp.zeros((V, 128), jnp.float32)
    for s in range(NB):
        row = tail[s].astype(jnp.float32)
        direction = jnp.where(which == s, rolled(row, LANES * s), direction)
        rotated = jnp.where(which == s, rolled(row, LANES * (s - 1)), rotated)
    last[0] = direction.astype(jnp.bfloat16)
    last[1] = rotated.astype(jnp.bfloat16)
    for k, ref in enumerate((d_ref, r_ref)):
        copies.append(pltpu.make_async_copy(last.at[k], ref.at[ROWS - 1], last_sems.at[k]))
        copies[-1].start()
    for c in copies:
        c.wait()


def unpack(parts):
    whole = jax.ShapeDtypeStruct((ROWS, V, 128), jnp.bfloat16)
    return pl.pallas_call(
        unpack_kernel,
        out_shape=(whole, whole),
        in_specs=[ANY],
        out_specs=(ANY, ANY),
        scratch_shapes=[
            pltpu.VMEM((NB, V, 128), jnp.bfloat16),
            pltpu.VMEM((2, V, 128), jnp.bfloat16),
            pltpu.SemaphoreType.DMA((2 * NB,)),
            pltpu.SemaphoreType.DMA((NB,)),
            pltpu.SemaphoreType.DMA((2,)),
        ],
        compiler_params=pltpu.CompilerParams(vmem_limit_bytes=VMEM_LIMIT),
        name="unpack",
    )(parts)


NZ, NY = 3, 9
VB = 16


def curl_kernel(eps_ref, mat_ref, w_ref, above_ref, below_ref, out_ref, tensor, electric):
    @pl.when(pl.program_id(0) == 0)
    def _():
        marks = mat_ref[...]
        for c in range(3):
            for d in range(3):
                value = jnp.full(marks.shape, eps_ref[0, c * 3 + d], jnp.float32)
                for m in range(1, NMAT):
                    value = jnp.where(marks == m, eps_ref[m, c * 3 + d], value)
                tensor[c * 3 + d] = 0.25 * value

    def field(c, z, y):
        y %= NY
        if z < 0:
            tile = below_ref[c * NY + y]
        elif z < NZ:
            tile = w_ref[(c * NZ + z) * NY + y]
        else:
            tile = above_ref[c * NY + y]
        return tile.astype(jnp.float32)

    for z in range(-1, NZ):
        for y in range(NY):
            hx, hy, hz = (field(c, z, y) for c in range(3))
            curl = (
                (field(2, z, y + 1) - hz) - (field(1, z + 1, y) - hy),
                (field(0, z + 1, y) - hx) - (rolled(hz, -1) - hz),
                (rolled(hy, -1) - hy) - (field(0, z, y + 1) - hx),
            )
            for c in range(3 if z >= 0 else 2):
                total = None
                for d in range(3):
                    weight = tensor[c * 3 + d, pl.ds((z + 1) * NY + y, 1)]
                    term = weight * curl[d]
                    total = term if total is None else total + term
                electric[c, (z + 1) * NY + y] = total
    for z in range(NZ):
        for y in range(NY):
            before = (y - 1) % NY
            here = (z + 1) * NY
            ex, ey, ez = (electric[c, here + y] for c in range(3))
            applied = (
                (ez - electric[2, here + before]) - (ey - electric[1, here + y - NY]),
                (ex - electric[0, here + y - NY]) - (ez - rolled(ez, 1)),
                (ey - rolled(ey, 1)) - (ex - electric[0, here + before]),
            )
            for c in range(3):
                out_ref[(c * NZ + z) * NY + y] = applied[c].astype(jnp.bfloat16)


def apply_curls(w, above, below, marks, eps):
    block = lambda rows: pl.BlockSpec((rows, VB, 128), lambda i: (0, i, 0))
    return pl.pallas_call(
        curl_kernel,
        out_shape=jax.ShapeDtypeStruct((ROWS, V, 128), jnp.bfloat16),
        grid=(V // VB,),
        in_specs=[
            pl.BlockSpec(memory_space=pltpu.SMEM),
            pl.BlockSpec(memory_space=pltpu.VMEM),
            block(ROWS),
            block(2 * NY),
            block(3 * NY),
        ],
        out_specs=block(ROWS),
        scratch_shapes=[
            pltpu.VMEM((9, (NZ + 1) * NY, 128), jnp.float32),
            pltpu.VMEM((3, (NZ + 1) * NY, VB, 128), jnp.float32),
        ],
        compiler_params=pltpu.CompilerParams(vmem_limit_bytes=VMEM_LIMIT),
        cost_estimate=pl.CostEstimate(
            flops=60_000_000, bytes_accessed=5_000_000, transcendentals=0
        ),
        name="curls",
    )(eps, marks, w, above, below)


def as_rows(x):
    return x.transpose(1, 2, 3, 0, 4).reshape(ROWS, V, 128)


def as_block(rows):
    return rows.reshape(3, NZ, NY, V, 128).transpose(3, 0, 1, 2, 4)


def per_device(current, search, previous, coefficients, material, inverse_permittivity):
    w, p, x = as_rows(search), as_rows(previous), as_rows(current)
    layers = w.reshape(3, NZ, NY, V, 128)
    above = ring_shift(layers[:2, 0].reshape(2 * NY, V, 128), "slab", -1)
    below = ring_shift(layers[:, NZ - 1].reshape(3 * NY, V, 128), "slab", 1)
    mark_below = ring_shift(material[NZ - 1 :], "slab", 1)
    marks = jnp.concatenate([mark_below, material]).reshape((NZ + 1) * NY, 128)
    packed = pack(w, p, x)
    cells = lax.all_to_all(packed, "blk", split_axis=0, concat_axis=0, tiled=True)
    coef = gather_coefficients(coefficients)
    parts = rotate(cells, coef)
    back = lax.all_to_all(parts, "blk", split_axis=0, concat_axis=0, tiled=True)
    applied = apply_curls(w, above, below, marks, inverse_permittivity.reshape(NMAT, 9))
    direction, rotated = unpack(back)
    return as_block(applied), as_block(rotated), as_block(direction)


def solution(mesh):
    block = P("blk", None, "slab", None, None)
    return jax.shard_map(
        per_device,
        mesh=mesh,
        in_specs=(block, block, block, P("slab", "blk"), P("slab", None, None), P()),
        out_specs=(block, block, block),
        check_vma=False,
    )
```

```python
import functools
import itertools

import jax
import jax.numpy as jnp
from jax import lax
from jax.experimental import pallas as pl
from jax.experimental.pallas import tpu as pltpu
from jax.sharding import PartitionSpec as P

M = 768
NMAT = 4
V = 96
NB = 8
ROWS = 81
SHARE = 10
LANES = 128 // NB
SLAB = (2, 8, 2)
BLK = (4, 2)
ANY = pl.BlockSpec(memory_space=pl.ANY)
VMEM_LIMIT = 56 * 1024 * 1024


def move(x, axis, sizes, steps):
    pairs = []
    for place in itertools.product(*[range(n) for n in sizes]):
        src = dst = 0
        for n, p, s in zip(sizes, place, steps):
            src = src * n + p
            dst = dst * n + (p + s) % n
        pairs.append((src, dst))
    return lax.ppermute(x, axis, pairs)


def ring_shift(x, axis, by):
    count = lax.axis_size(axis)
    return lax.ppermute(x, axis, [(i, (i + by) % count) for i in range(count)])


def gather_plane(tile):
    pieces = [tile]
    pieces.append(move(tile, "blk", BLK, (0, 1)))
    pieces.append(move(tile, "slab", SLAB, (1, 0, 0)))
    pieces.append(
        lax.ppermute(
            tile,
            ("slab", "blk"),
            [
                (s * NB + b, (s + 16) % 32 * NB + (b ^ 1))
                for s in range(32)
                for b in range(NB)
            ],
        )
    )
    t = jnp.stack(pieces)
    return jnp.stack([t] + [move(t, "blk", BLK, (-k, 0)) for k in (1, 2, 3)])


def gather_coefficients(plane):
    slab, blk = lax.axis_index("slab"), lax.axis_index("blk")
    place = jnp.stack([slab // 16, (slab // 2) % 8, slab % 2, blk // 2, blk % 2])
    groups = [[h * 16 + z * 2 + c for z in range(8)] for h in range(2) for c in range(2)]
    mine = lax.all_gather(plane, "slab", axis_index_groups=groups)
    other = move(mine, "slab", SLAB, (0, 0, 1))
    return assemble(place, mine, other)


def assemble_kernel(place_ref, mine_ref, other_ref, out_ref):
    here, core = place_ref[0], place_ref[2]
    tiles = []
    for y_hi in range(2):
        k = (y_hi - here + 2) % 2
        for z in range(8):
            own = mine_ref[z, 0, k, 0].astype(jnp.float32)
            far = other_ref[z, 0, k, 0].astype(jnp.float32)
            tiles.append(jnp.where(core == 0, own, far))
            tiles.append(jnp.where(core == 0, far, own))
    out_ref[...] = jnp.concatenate(tiles, axis=0).T.astype(jnp.bfloat16)


def assemble(place, mine, other):
    def piece(b, at):
        return 0, (b // 2 - at[3] + 4) % 4, 0, (b % 2 - at[4] + 2) % 2, 0, 0

    mine, other = (t.reshape(8, 4, 2, 2, 72, 96) for t in (mine, other))
    pieces = pl.BlockSpec((8, 1, 2, 1, 72, 96), piece)
    return pl.pallas_call(
        assemble_kernel,
        out_shape=jax.ShapeDtypeStruct((M, 3 * M), jnp.bfloat16),
        grid_spec=pltpu.PrefetchScalarGridSpec(
            num_scalar_prefetch=1,
            grid=(NB,),
            in_specs=[pieces, pieces],
            out_specs=pl.BlockSpec((M // NB, 3 * M), lambda b, at: (b, 0)),
        ),
        compiler_params=pltpu.CompilerParams(vmem_limit_bytes=VMEM_LIMIT),
        cost_estimate=pl.CostEstimate(
            flops=10_000_000, bytes_accessed=8_000_000, transcendentals=0
        ),
        name="assemble",
    )(place, mine, other)


def lane_index(shape):
    return lax.broadcasted_iota(jnp.int32, shape, len(shape) - 1)


def rolled(x, by):
    by %= 128
    return x if by == 0 else pltpu.roll(x, by, x.ndim - 1)


def pack_kernel(w_ref, p_ref, x_ref, out_ref, stage, tail, in_sems, tail_sems, out_sems):
    fields = (w_ref, p_ref, x_ref)
    last = [
        pltpu.make_async_copy(ref.at[ROWS - 1], tail.at[k], tail_sems.at[k])
        for k, ref in enumerate(fields)
    ]
    fetches = [
        [
            pltpu.make_async_copy(
                ref.at[pl.ds(SHARE * d, SHARE)],
                stage.at[d, pl.ds(SHARE * k, SHARE)],
                in_sems.at[d, k],
            )
            for k, ref in enumerate(fields)
        ]
        for d in range(NB)
    ]
    sends = [
        pltpu.make_async_copy(stage.at[d], out_ref.at[d], out_sems.at[d])
        for d in range(NB)
    ]
    for c in last:
        c.start()
    for group in fetches:
        for c in group:
            c.start()
    for c in last:
        c.wait()
    lane = lane_index((V, 128))
    w, p, x = (tail[k].astype(jnp.float32) for k in range(3))
    for d in range(NB):
        row = jnp.where(lane < 3 * LANES, rolled(x, LANES * (2 - d)), 0.0)
        row = jnp.where(lane < 2 * LANES, rolled(p, LANES * (1 - d)), row)
        row = jnp.where(lane < LANES, rolled(w, LANES * (0 - d)), row)
        stage[d, 3 * SHARE] = row.astype(jnp.bfloat16)
        for c in fetches[d]:
            c.wait()
        sends[d].start()
    for c in sends:
        c.wait()


def pack(w, p, x):
    shape = (NB, 3 * SHARE + 1, V, 128)
    return pl.pallas_call(
        pack_kernel,
        out_shape=jax.ShapeDtypeStruct(shape, jnp.bfloat16),
        in_specs=[ANY] * 3,
        out_specs=ANY,
        scratch_shapes=[
            pltpu.VMEM(shape, jnp.bfloat16),
            pltpu.VMEM((3, V, 128), jnp.bfloat16),
            pltpu.SemaphoreType.DMA((NB, 3)),
            pltpu.SemaphoreType.DMA((3,)),
            pltpu.SemaphoreType.DMA((NB,)),
        ],
        compiler_params=pltpu.CompilerParams(vmem_limit_bytes=VMEM_LIMIT),
        cost_estimate=pl.CostEstimate(
            flops=2_000_000, bytes_accessed=12_000_000, transcendentals=0
        ),
        name="pack",
    )(w, p, x)


def rotate_kernel(cells_ref, coef_ref, out_ref, cells, out, in_sems, out_sems):
    def fetch(k, i):
        rows = pl.ds(SHARE * k + 2 * i, 2)
        return pltpu.make_async_copy(
            cells_ref.at[:, rows], cells.at[:, rows], in_sems.at[k, i]
        )

    def put(k, i):
        rows = pl.ds(SHARE * k + 2 * i, 2)
        return pltpu.make_async_copy(
            out.at[:, rows], out_ref.at[:, rows], out_sems.at[k, i]
        )

    steps = SHARE // 2
    fetch_tail = pltpu.make_async_copy(
        cells_ref.at[:, pl.ds(3 * SHARE, 1)],
        cells.at[:, pl.ds(3 * SHARE, 1)],
        in_sems.at[0, steps],
    )
    put_tail = pltpu.make_async_copy(
        out.at[:, pl.ds(2 * SHARE, 1)],
        out_ref.at[:, pl.ds(2 * SHARE, 1)],
        out_sems.at[0, steps],
    )
    for i in range(steps):
        for k in range(3):
            fetch(k, i).start()
    fetch_tail.start()

    def product(w, p, x):
        wp = jnp.concatenate([w, p], axis=0)
        direction = jnp.dot(
            coef_ref[:, M:], wp, preferred_element_type=jnp.float32
        )
        rotated = direction + jnp.dot(
            coef_ref[:, :M], x, preferred_element_type=jnp.float32
        )
        return direction, rotated

    def step(i, carry):
        for k in range(3):
            fetch(k, i).wait()

        def row_pair(k):
            first = cells[:, SHARE * k + 2 * i].reshape(M, 128)
            second = cells[:, SHARE * k + 2 * i + 1].reshape(M, 128)
            return jnp.concatenate([first, second], axis=1)

        results = product(row_pair(0), row_pair(1), row_pair(2))
        for k, result in enumerate(results):
            result = result.astype(jnp.bfloat16)
            for j in range(2):
                part = result[:, 128 * j : 128 * (j + 1)]
                out[:, SHARE * k + 2 * i + j] = part.reshape(NB, V, 128)
            put(k, i).start()
        return carry

    lax.fori_loop(0, steps, step, 0)
    fetch_tail.wait()
    tail = cells[:, 3 * SHARE].reshape(M, 128)
    wide = tail.astype(jnp.float32)
    shifted = [rolled(wide, -LANES * k).astype(jnp.bfloat16) for k in (1, 2)]
    direction, rotated = product(tail, *shifted)
    mixed = jnp.where(
        lane_index((M, 128)) < LANES, direction, rolled(rotated, LANES)
    )
    out[:, 2 * SHARE] = mixed.astype(jnp.bfloat16).reshape(NB, V, 128)
    put_tail.start()
    for k in range(2):
        for i in range(steps):
            put(k, i).wait()
    put_tail.wait()


def rotate(cells, coef):
    return pl.pallas_call(
        rotate_kernel,
        out_shape=jax.ShapeDtypeStruct((NB, 2 * SHARE + 1, V, 128), jnp.bfloat16),
        in_specs=[ANY, pl.BlockSpec(memory_space=pltpu.VMEM)],
        out_specs=ANY,
        scratch_shapes=[
            pltpu.VMEM((NB, 3 * SHARE + 1, V, 128), jnp.bfloat16),
            pltpu.VMEM((NB, 2 * SHARE + 1, V, 128), jnp.bfloat16),
            pltpu.SemaphoreType.DMA((3, SHARE // 2 + 1)),
            pltpu.SemaphoreType.DMA((2, SHARE // 2 + 1)),
        ],
        compiler_params=pltpu.CompilerParams(vmem_limit_bytes=VMEM_LIMIT),
        cost_estimate=pl.CostEstimate(
            flops=6 * M * M * 128 * (SHARE + 1), bytes_accessed=14_000_000, transcendentals=0
        ),
        name="rotate",
    )(cells, coef)


def unpack_kernel(in_ref, d_ref, r_ref, stage, last, in_sems, tail_sems, out_sems, last_sems):
    tails = [
        pltpu.make_async_copy(
            in_ref.at[s, 2 * SHARE], stage.at[s, 2 * SHARE], tail_sems.at[s]
        )
        for s in range(NB)
    ]
    fetches = [
        pltpu.make_async_copy(
            in_ref.at[s, pl.ds(0, 2 * SHARE)],
            stage.at[s, pl.ds(0, 2 * SHARE)],
            in_sems.at[s],
        )
        for s in range(NB)
    ]
    for c in tails + fetches:
        c.start()
    for c in tails:
        c.wait()
    which = lane_index((V, 128)) // LANES
    direction = rotated = jnp.zeros((V, 128), jnp.float32)
    copies = []
    for s in range(NB):
        row = stage[s, 2 * SHARE].astype(jnp.float32)
        direction = jnp.where(which == s, rolled(row, LANES * s), direction)
        rotated = jnp.where(which == s, rolled(row, LANES * (s - 1)), rotated)
        fetches[s].wait()
        for k, ref in enumerate((d_ref, r_ref)):
            copies.append(
                pltpu.make_async_copy(
                    stage.at[s, pl.ds(SHARE * k, SHARE)],
                    ref.at[pl.ds(SHARE * s, SHARE)],
                    out_sems.at[s, k],
                )
            )
            copies[-1].start()
    last[0] = direction.astype(jnp.bfloat16)
    last[1] = rotated.astype(jnp.bfloat16)
    for k, ref in enumerate((d_ref, r_ref)):
        copies.append(pltpu.make_async_copy(last.at[k], ref.at[ROWS - 1], last_sems.at[k]))
        copies[-1].start()
    for c in copies:
        c.wait()


def unpack(parts):
    whole = jax.ShapeDtypeStruct((ROWS, V, 128), jnp.bfloat16)
    return pl.pallas_call(
        unpack_kernel,
        out_shape=(whole, whole),
        in_specs=[ANY],
        out_specs=(ANY, ANY),
        scratch_shapes=[
            pltpu.VMEM((NB, 2 * SHARE + 1, V, 128), jnp.bfloat16),
            pltpu.VMEM((2, V, 128), jnp.bfloat16),
            pltpu.SemaphoreType.DMA((NB,)),
            pltpu.SemaphoreType.DMA((NB,)),
            pltpu.SemaphoreType.DMA((NB, 2)),
            pltpu.SemaphoreType.DMA((2,)),
        ],
        compiler_params=pltpu.CompilerParams(vmem_limit_bytes=VMEM_LIMIT),
        name="unpack",
    )(parts)


NZ, NY = 3, 9
VB = 16


def curl_kernel(eps_ref, mat_ref, w_ref, above_ref, below_ref, out_ref, tensor, electric):
    @pl.when(pl.program_id(0) == 0)
    def _():
        marks = mat_ref[...]
        for c in range(3):
            for d in range(3):
                value = jnp.full(marks.shape, eps_ref[0, c * 3 + d], jnp.float32)
                for m in range(1, NMAT):
                    value = jnp.where(marks == m, eps_ref[m, c * 3 + d], value)
                tensor[c * 3 + d] = 0.25 * value

    def field(c, z, y):
        y %= NY
        if z < 0:
            tile = below_ref[c * NY + y]
        elif z < NZ:
            tile = w_ref[(c * NZ + z) * NY + y]
        else:
            tile = above_ref[c * NY + y]
        return tile.astype(jnp.float32)

    for z in range(-1, NZ):
        for y in range(NY):
            hx, hy, hz = (field(c, z, y) for c in range(3))
            curl = (
                (field(2, z, y + 1) - hz) - (field(1, z + 1, y) - hy),
                (field(0, z + 1, y) - hx) - (rolled(hz, -1) - hz),
                (rolled(hy, -1) - hy) - (field(0, z, y + 1) - hx),
            )
            for c in range(3 if z >= 0 else 2):
                total = None
                for d in range(3):
                    weight = tensor[c * 3 + d, pl.ds((z + 1) * NY + y, 1)]
                    term = weight * curl[d]
                    total = term if total is None else total + term
                electric[c, (z + 1) * NY + y] = total
    for z in range(NZ):
        for y in range(NY):
            before = (y - 1) % NY
            here = (z + 1) * NY
            ex, ey, ez = (electric[c, here + y] for c in range(3))
            applied = (
                (ez - electric[2, here + before]) - (ey - electric[1, here + y - NY]),
                (ex - electric[0, here + y - NY]) - (ez - rolled(ez, 1)),
                (ey - rolled(ey, 1)) - (ex - electric[0, here + before]),
            )
            for c in range(3):
                out_ref[(c * NZ + z) * NY + y] = applied[c].astype(jnp.bfloat16)


def apply_curls(w, above, below, marks, eps):
    block = lambda rows: pl.BlockSpec((rows, VB, 128), lambda i: (0, i, 0))
    return pl.pallas_call(
        curl_kernel,
        out_shape=jax.ShapeDtypeStruct((ROWS, V, 128), jnp.bfloat16),
        grid=(V // VB,),
        in_specs=[
            pl.BlockSpec(memory_space=pltpu.SMEM),
            pl.BlockSpec(memory_space=pltpu.VMEM),
            block(ROWS),
            block(2 * NY),
            block(3 * NY),
        ],
        out_specs=block(ROWS),
        scratch_shapes=[
            pltpu.VMEM((9, (NZ + 1) * NY, 128), jnp.float32),
            pltpu.VMEM((3, (NZ + 1) * NY, VB, 128), jnp.float32),
        ],
        compiler_params=pltpu.CompilerParams(vmem_limit_bytes=VMEM_LIMIT),
        cost_estimate=pl.CostEstimate(
            flops=60_000_000, bytes_accessed=5_000_000, transcendentals=0
        ),
        name="curls",
    )(eps, marks, w, above, below)


def as_rows(x):
    return x.transpose(1, 2, 3, 0, 4).reshape(ROWS, V, 128)


def as_block(rows):
    return rows.reshape(3, NZ, NY, V, 128).transpose(3, 0, 1, 2, 4)


def per_device(current, search, previous, coefficients, material, inverse_permittivity):
    w, p, x = as_rows(search), as_rows(previous), as_rows(current)
    packed = pack(w, p, x)
    plane = gather_plane(coefficients)
    packed, plane = lax.optimization_barrier((packed, plane))
    cells = lax.all_to_all(packed, "blk", split_axis=0, concat_axis=0, tiled=True)
    layers = w.reshape(3, NZ, NY, V, 128)
    above = ring_shift(layers[:2, 0].reshape(2 * NY, V, 128), "slab", -1)
    below = ring_shift(layers[:, NZ - 1].reshape(3 * NY, V, 128), "slab", 1)
    mark_below = ring_shift(material[NZ - 1 :], "slab", 1)
    plane, below, mark_below = lax.optimization_barrier((plane, below, mark_below))
    marks = jnp.concatenate([mark_below, material]).reshape((NZ + 1) * NY, 128)
    coef = gather_coefficients(plane)
    coef, above = lax.optimization_barrier((coef, above))
    parts = rotate(cells, coef)
    back = lax.all_to_all(parts, "blk", split_axis=0, concat_axis=0, tiled=True)
    applied = apply_curls(w, above, below, marks, inverse_permittivity.reshape(NMAT, 9))
    direction, rotated = unpack(back)
    return as_block(applied), as_block(rotated), as_block(direction)


def solution(mesh):
    block = P("blk", None, "slab", None, None)
    return jax.shard_map(
        per_device,
        mesh=mesh,
        in_specs=(block, block, block, P("slab", "blk"), P("slab", None, None), P()),
        out_specs=(block, block, block),
        check_vma=False,
    )
```

```python
import functools
import itertools

import jax
import jax.numpy as jnp
from jax import lax
from jax.experimental import pallas as pl
from jax.experimental.pallas import tpu as pltpu
from jax.sharding import PartitionSpec as P

M = 768
NMAT = 4
V = 96
NB = 8
ROWS = 81
SHARE = 10
LANES = 128 // NB
SLAB = (2, 8, 2)
BLK = (4, 2)
ANY = pl.BlockSpec(memory_space=pl.ANY)
VMEM_LIMIT = 56 * 1024 * 1024


def move(x, axis, sizes, steps):
    pairs = []
    for place in itertools.product(*[range(n) for n in sizes]):
        src = dst = 0
        for n, p, s in zip(sizes, place, steps):
            src = src * n + p
            dst = dst * n + (p + s) % n
        pairs.append((src, dst))
    return lax.ppermute(x, axis, pairs)


def ring_shift(x, axis, by):
    count = lax.axis_size(axis)
    return lax.ppermute(x, axis, [(i, (i + by) % count) for i in range(count)])


def gather_plane(tile):
    pieces = [tile]
    pieces.append(move(tile, "blk", BLK, (0, 1)))
    pieces.append(move(tile, "slab", SLAB, (1, 0, 0)))
    pieces.append(
        lax.ppermute(
            tile,
            ("slab", "blk"),
            [
                (s * NB + b, (s + 16) % 32 * NB + (b ^ 1))
                for s in range(32)
                for b in range(NB)
            ],
        )
    )
    t = jnp.stack(pieces)
    return jnp.stack([t] + [move(t, "blk", BLK, (-k, 0)) for k in (1, 2, 3)])


def assemble_kernel(place_ref, mine_ref, other_ref, out_ref):
    here, core = place_ref[0], place_ref[2]
    tiles = []
    for y_hi in range(2):
        k = (y_hi - here + 2) % 2
        for z in range(8):
            own = mine_ref[z, 0, k, 0].astype(jnp.float32)
            far = other_ref[z, 0, k, 0].astype(jnp.float32)
            tiles.append(jnp.where(core == 0, own, far))
            tiles.append(jnp.where(core == 0, far, own))
    out_ref[...] = jnp.concatenate(tiles, axis=0).T.astype(jnp.bfloat16)


def assemble(place, mine, other):
    def piece(b, at):
        return 0, (b // 2 - at[3] + 4) % 4, 0, (b % 2 - at[4] + 2) % 2, 0, 0

    mine, other = (t.reshape(8, 4, 2, 2, 72, 96) for t in (mine, other))
    pieces = pl.BlockSpec((8, 1, 2, 1, 72, 96), piece)
    return pl.pallas_call(
        assemble_kernel,
        out_shape=jax.ShapeDtypeStruct((M, 3 * M), jnp.bfloat16),
        grid_spec=pltpu.PrefetchScalarGridSpec(
            num_scalar_prefetch=1,
            grid=(NB,),
            in_specs=[pieces, pieces],
            out_specs=pl.BlockSpec((M // NB, 3 * M), lambda b, at: (b, 0)),
        ),
        compiler_params=pltpu.CompilerParams(vmem_limit_bytes=VMEM_LIMIT),
        cost_estimate=pl.CostEstimate(
            flops=10_000_000, bytes_accessed=8_000_000, transcendentals=0
        ),
        name="assemble",
    )(place, mine, other)


def lane_index(shape):
    return lax.broadcasted_iota(jnp.int32, shape, len(shape) - 1)


def rolled(x, by):
    by %= 128
    return x if by == 0 else pltpu.roll(x, by, x.ndim - 1)


def pack_kernel(w_ref, p_ref, x_ref, out_ref, stage, tail, in_sems, tail_sems, out_sems):
    fields = (w_ref, p_ref, x_ref)
    last = [
        pltpu.make_async_copy(ref.at[ROWS - 1], tail.at[k], tail_sems.at[k])
        for k, ref in enumerate(fields)
    ]
    fetches = [
        [
            pltpu.make_async_copy(
                ref.at[pl.ds(SHARE * d, SHARE)],
                stage.at[d, pl.ds(SHARE * k, SHARE)],
                in_sems.at[d, k],
            )
            for k, ref in enumerate(fields)
        ]
        for d in range(NB)
    ]
    sends = [
        pltpu.make_async_copy(stage.at[d], out_ref.at[d], out_sems.at[d])
        for d in range(NB)
    ]
    for c in last:
        c.start()
    for group in fetches:
        for c in group:
            c.start()
    for c in last:
        c.wait()
    lane = lane_index((V, 128))
    w, p, x = (tail[k].astype(jnp.float32) for k in range(3))
    for d in range(NB):
        row = jnp.where(lane < 3 * LANES, rolled(x, LANES * (2 - d)), 0.0)
        row = jnp.where(lane < 2 * LANES, rolled(p, LANES * (1 - d)), row)
        row = jnp.where(lane < LANES, rolled(w, LANES * (0 - d)), row)
        stage[d, 3 * SHARE] = row.astype(jnp.bfloat16)
        for c in fetches[d]:
            c.wait()
        sends[d].start()
    for c in sends:
        c.wait()


def pack(w, p, x):
    shape = (NB, 3 * SHARE + 1, V, 128)
    return pl.pallas_call(
        pack_kernel,
        out_shape=jax.ShapeDtypeStruct(shape, jnp.bfloat16),
        in_specs=[ANY] * 3,
        out_specs=ANY,
        scratch_shapes=[
            pltpu.VMEM(shape, jnp.bfloat16),
            pltpu.VMEM((3, V, 128), jnp.bfloat16),
            pltpu.SemaphoreType.DMA((NB, 3)),
            pltpu.SemaphoreType.DMA((3,)),
            pltpu.SemaphoreType.DMA((NB,)),
        ],
        compiler_params=pltpu.CompilerParams(vmem_limit_bytes=VMEM_LIMIT),
        cost_estimate=pl.CostEstimate(
            flops=2_000_000, bytes_accessed=12_000_000, transcendentals=0
        ),
        name="pack",
    )(w, p, x)


def rotate_kernel(cells_ref, coef_ref, after_ref, out_ref, cells, out, in_sems, out_sems):
    del after_ref

    def fetch(k, i):
        rows = pl.ds(SHARE * k + 2 * i, 2)
        return pltpu.make_async_copy(
            cells_ref.at[:, rows], cells.at[:, rows], in_sems.at[k, i]
        )

    def put(k, i):
        rows = pl.ds(SHARE * k + 2 * i, 2)
        return pltpu.make_async_copy(
            out.at[:, rows], out_ref.at[:, rows], out_sems.at[k, i]
        )

    steps = SHARE // 2
    fetch_tail = pltpu.make_async_copy(
        cells_ref.at[:, pl.ds(3 * SHARE, 1)],
        cells.at[:, pl.ds(3 * SHARE, 1)],
        in_sems.at[0, steps],
    )
    put_tail = pltpu.make_async_copy(
        out.at[:, pl.ds(2 * SHARE, 1)],
        out_ref.at[:, pl.ds(2 * SHARE, 1)],
        out_sems.at[0, steps],
    )
    for i in range(steps):
        for k in range(3):
            fetch(k, i).start()
    fetch_tail.start()

    def product(w, p, x):
        wp = jnp.concatenate([w, p], axis=0)
        direction = jnp.dot(
            coef_ref[:, M:], wp, preferred_element_type=jnp.float32
        )
        rotated = direction + jnp.dot(
            coef_ref[:, :M], x, preferred_element_type=jnp.float32
        )
        return direction, rotated

    def step(i, carry):
        for k in range(3):
            fetch(k, i).wait()

        def row_pair(k):
            first = cells[:, SHARE * k + 2 * i].reshape(M, 128)
            second = cells[:, SHARE * k + 2 * i + 1].reshape(M, 128)
            return jnp.concatenate([first, second], axis=1)

        results = product(row_pair(0), row_pair(1), row_pair(2))
        for k, result in enumerate(results):
            result = result.astype(jnp.bfloat16)
            for j in range(2):
                part = result[:, 128 * j : 128 * (j + 1)]
                out[:, SHARE * k + 2 * i + j] = part.reshape(NB, V, 128)
            put(k, i).start()
        return carry

    lax.fori_loop(0, steps, step, 0)
    fetch_tail.wait()
    tail = cells[:, 3 * SHARE].reshape(M, 128)
    wide = tail.astype(jnp.float32)
    shifted = [rolled(wide, -LANES * k).astype(jnp.bfloat16) for k in (1, 2)]
    direction, rotated = product(tail, *shifted)
    mixed = jnp.where(
        lane_index((M, 128)) < LANES, direction, rolled(rotated, LANES)
    )
    out[:, 2 * SHARE] = mixed.astype(jnp.bfloat16).reshape(NB, V, 128)
    put_tail.start()
    for k in range(2):
        for i in range(steps):
            put(k, i).wait()
    put_tail.wait()


def rotate(cells, coef, after):
    return pl.pallas_call(
        rotate_kernel,
        out_shape=jax.ShapeDtypeStruct((NB, 2 * SHARE + 1, V, 128), jnp.bfloat16),
        in_specs=[ANY, pl.BlockSpec(memory_space=pltpu.VMEM), ANY],
        out_specs=ANY,
        scratch_shapes=[
            pltpu.VMEM((NB, 3 * SHARE + 1, V, 128), jnp.bfloat16),
            pltpu.VMEM((NB, 2 * SHARE + 1, V, 128), jnp.bfloat16),
            pltpu.SemaphoreType.DMA((3, SHARE // 2 + 1)),
            pltpu.SemaphoreType.DMA((2, SHARE // 2 + 1)),
        ],
        compiler_params=pltpu.CompilerParams(vmem_limit_bytes=VMEM_LIMIT),
        cost_estimate=pl.CostEstimate(
            flops=6 * M * M * 128 * (SHARE + 1), bytes_accessed=14_000_000, transcendentals=0
        ),
        name="rotate",
    )(cells, coef, after)


def unpack_kernel(in_ref, d_ref, r_ref, stage, last, in_sems, tail_sems, out_sems, last_sems):
    tails = [
        pltpu.make_async_copy(
            in_ref.at[s, 2 * SHARE], stage.at[s, 2 * SHARE], tail_sems.at[s]
        )
        for s in range(NB)
    ]
    fetches = [
        pltpu.make_async_copy(
            in_ref.at[s, pl.ds(0, 2 * SHARE)],
            stage.at[s, pl.ds(0, 2 * SHARE)],
            in_sems.at[s],
        )
        for s in range(NB)
    ]
    for c in tails + fetches:
        c.start()
    for c in tails:
        c.wait()
    which = lane_index((V, 128)) // LANES
    direction = rotated = jnp.zeros((V, 128), jnp.float32)
    copies = []
    for s in range(NB):
        row = stage[s, 2 * SHARE].astype(jnp.float32)
        direction = jnp.where(which == s, rolled(row, LANES * s), direction)
        rotated = jnp.where(which == s, rolled(row, LANES * (s - 1)), rotated)
        fetches[s].wait()
        for k, ref in enumerate((d_ref, r_ref)):
            copies.append(
                pltpu.make_async_copy(
                    stage.at[s, pl.ds(SHARE * k, SHARE)],
                    ref.at[pl.ds(SHARE * s, SHARE)],
                    out_sems.at[s, k],
                )
            )
            copies[-1].start()
    last[0] = direction.astype(jnp.bfloat16)
    last[1] = rotated.astype(jnp.bfloat16)
    for k, ref in enumerate((d_ref, r_ref)):
        copies.append(pltpu.make_async_copy(last.at[k], ref.at[ROWS - 1], last_sems.at[k]))
        copies[-1].start()
    for c in copies:
        c.wait()


def unpack(parts):
    whole = jax.ShapeDtypeStruct((ROWS, V, 128), jnp.bfloat16)
    return pl.pallas_call(
        unpack_kernel,
        out_shape=(whole, whole),
        in_specs=[ANY],
        out_specs=(ANY, ANY),
        scratch_shapes=[
            pltpu.VMEM((NB, 2 * SHARE + 1, V, 128), jnp.bfloat16),
            pltpu.VMEM((2, V, 128), jnp.bfloat16),
            pltpu.SemaphoreType.DMA((NB,)),
            pltpu.SemaphoreType.DMA((NB,)),
            pltpu.SemaphoreType.DMA((NB, 2)),
            pltpu.SemaphoreType.DMA((2,)),
        ],
        compiler_params=pltpu.CompilerParams(vmem_limit_bytes=VMEM_LIMIT),
        name="unpack",
    )(parts)


def hold(arrays, until):
    count = len(arrays)

    def kernel(*refs):
        del refs

    return pl.pallas_call(
        kernel,
        out_shape=[jax.ShapeDtypeStruct(x.shape, x.dtype) for x in arrays],
        in_specs=[ANY] * (count + len(until)),
        out_specs=[ANY] * count,
        input_output_aliases={i: i for i in range(count)},
        name="hold",
    )(*arrays, *until)


NZ, NY = 3, 9
VB = 16


def curl_kernel(eps_ref, mat_ref, w_ref, above_ref, below_ref, out_ref, tensor, electric):
    @pl.when(pl.program_id(0) == 0)
    def _():
        marks = mat_ref[...]
        for c in range(3):
            for d in range(3):
                value = jnp.full(marks.shape, eps_ref[0, c * 3 + d], jnp.float32)
                for m in range(1, NMAT):
                    value = jnp.where(marks == m, eps_ref[m, c * 3 + d], value)
                tensor[c * 3 + d] = 0.25 * value

    def field(c, z, y):
        y %= NY
        if z < 0:
            tile = below_ref[c * NY + y]
        elif z < NZ:
            tile = w_ref[(c * NZ + z) * NY + y]
        else:
            tile = above_ref[c * NY + y]
        return tile.astype(jnp.float32)

    for z in range(-1, NZ):
        for y in range(NY):
            hx, hy, hz = (field(c, z, y) for c in range(3))
            curl = (
                (field(2, z, y + 1) - hz) - (field(1, z + 1, y) - hy),
                (field(0, z + 1, y) - hx) - (rolled(hz, -1) - hz),
                (rolled(hy, -1) - hy) - (field(0, z, y + 1) - hx),
            )
            for c in range(3 if z >= 0 else 2):
                total = None
                for d in range(3):
                    weight = tensor[c * 3 + d, pl.ds((z + 1) * NY + y, 1)]
                    term = weight * curl[d]
                    total = term if total is None else total + term
                electric[c, (z + 1) * NY + y] = total
    for z in range(NZ):
        for y in range(NY):
            before = (y - 1) % NY
            here = (z + 1) * NY
            ex, ey, ez = (electric[c, here + y] for c in range(3))
            applied = (
                (ez - electric[2, here + before]) - (ey - electric[1, here + y - NY]),
                (ex - electric[0, here + y - NY]) - (ez - rolled(ez, 1)),
                (ey - rolled(ey, 1)) - (ex - electric[0, here + before]),
            )
            for c in range(3):
                out_ref[(c * NZ + z) * NY + y] = applied[c].astype(jnp.bfloat16)


def apply_curls(w, above, below, marks, eps):
    block = lambda rows: pl.BlockSpec((rows, VB, 128), lambda i: (0, i, 0))
    return pl.pallas_call(
        curl_kernel,
        out_shape=jax.ShapeDtypeStruct((ROWS, V, 128), jnp.bfloat16),
        grid=(V // VB,),
        in_specs=[
            pl.BlockSpec(memory_space=pltpu.SMEM),
            pl.BlockSpec(memory_space=pltpu.VMEM),
            block(ROWS),
            block(2 * NY),
            block(3 * NY),
        ],
        out_specs=block(ROWS),
        scratch_shapes=[
            pltpu.VMEM((9, (NZ + 1) * NY, 128), jnp.float32),
            pltpu.VMEM((3, (NZ + 1) * NY, VB, 128), jnp.float32),
        ],
        compiler_params=pltpu.CompilerParams(vmem_limit_bytes=VMEM_LIMIT),
        cost_estimate=pl.CostEstimate(
            flops=60_000_000, bytes_accessed=5_000_000, transcendentals=0
        ),
        name="curls",
    )(eps, marks, w, above, below)


def as_rows(x):
    return x.transpose(1, 2, 3, 0, 4).reshape(ROWS, V, 128)


def as_block(rows):
    return rows.reshape(3, NZ, NY, V, 128).transpose(3, 0, 1, 2, 4)


def per_device(current, search, previous, coefficients, material, inverse_permittivity):
    w, p, x = as_rows(search), as_rows(previous), as_rows(current)
    slab, blk = lax.axis_index("slab"), lax.axis_index("blk")
    place = jnp.stack([slab // 16, (slab // 2) % 8, slab % 2, blk // 2, blk % 2])
    mark_below = ring_shift(material[NZ - 1 :], "slab", 1)
    marks = jnp.concatenate([mark_below, material]).reshape((NZ + 1) * NY, 128)
    packed = pack(w, p, x)
    plane = gather_plane(coefficients)
    packed, plane = lax.optimization_barrier((packed, plane))
    cells = lax.all_to_all(packed, "blk", split_axis=0, concat_axis=0, tiled=True)
    groups = [[h * 16 + z * 2 + c for z in range(8)] for h in range(2) for c in range(2)]
    mine = lax.all_gather(plane, "slab", axis_index_groups=groups)
    other = move(mine, "slab", SLAB, (0, 0, 1))
    coef = assemble(place, mine, other)
    layers = w.reshape(3, NZ, NY, V, 128)
    low = layers[:2, 0].reshape(2 * NY, V, 128)
    high = layers[:, NZ - 1].reshape(3 * NY, V, 128)
    low, high = hold([low, high], [mine])
    above = ring_shift(low, "slab", -1)
    below = ring_shift(high, "slab", 1)
    applied = apply_curls(w, above, below, marks, inverse_permittivity.reshape(NMAT, 9))
    parts = rotate(cells, coef, applied)
    back = lax.all_to_all(parts, "blk", split_axis=0, concat_axis=0, tiled=True)
    direction, rotated = unpack(back)
    return as_block(applied), as_block(rotated), as_block(direction)


def solution(mesh):
    block = P("blk", None, "slab", None, None)
    return jax.shard_map(
        per_device,
        mesh=mesh,
        in_specs=(block, block, block, P("slab", "blk"), P("slab", None, None), P()),
        out_specs=(block, block, block),
        check_vma=False,
    )
```

```python
import functools
import itertools

import jax
import jax.numpy as jnp
from jax import lax
from jax.experimental import pallas as pl
from jax.experimental.pallas import tpu as pltpu
from jax.sharding import PartitionSpec as P

M = 768
NMAT = 4
V = 96
NB = 8
ROWS = 81
SHARE = 10
LANES = 128 // NB
SLAB = (2, 8, 2)
BLK = (4, 2)
ANY = pl.BlockSpec(memory_space=pl.ANY)
MIB = 1024 * 1024


def move(x, axis, sizes, steps):
    pairs = []
    for place in itertools.product(*[range(n) for n in sizes]):
        src = dst = 0
        for n, p, s in zip(sizes, place, steps):
            src = src * n + p
            dst = dst * n + (p + s) % n
        pairs.append((src, dst))
    return lax.ppermute(x, axis, pairs)


def ring_shift(x, axis, by):
    count = lax.axis_size(axis)
    return lax.ppermute(x, axis, [(i, (i + by) % count) for i in range(count)])


def gather_plane(tile):
    pieces = [tile]
    pieces.append(move(tile, "blk", BLK, (0, 1)))
    pieces.append(move(tile, "slab", SLAB, (1, 0, 0)))
    pieces.append(
        lax.ppermute(
            tile,
            ("slab", "blk"),
            [
                (s * NB + b, (s + 16) % 32 * NB + (b ^ 1))
                for s in range(32)
                for b in range(NB)
            ],
        )
    )
    t = jnp.stack(pieces)
    return jnp.stack([t] + [move(t, "blk", BLK, (-k, 0)) for k in (1, 2, 3)])


def assemble_kernel(place_ref, mine_ref, other_ref, out_ref):
    here, core = place_ref[0], place_ref[2]
    tiles = []
    for y_hi in range(2):
        k = (y_hi - here + 2) % 2
        for z in range(8):
            own = mine_ref[z, 0, k, 0].astype(jnp.float32)
            far = other_ref[z, 0, k, 0].astype(jnp.float32)
            tiles.append(jnp.where(core == 0, own, far))
            tiles.append(jnp.where(core == 0, far, own))
    out_ref[...] = jnp.concatenate(tiles, axis=0).T.astype(jnp.bfloat16)


def assemble(place, mine, other):
    def piece(b, at):
        return 0, (b // 2 - at[3] + 4) % 4, 0, (b % 2 - at[4] + 2) % 2, 0, 0

    mine, other = (t.reshape(8, 4, 2, 2, 72, 96) for t in (mine, other))
    pieces = pl.BlockSpec((8, 1, 2, 1, 72, 96), piece)
    return pl.pallas_call(
        assemble_kernel,
        out_shape=jax.ShapeDtypeStruct((M, 3 * M), jnp.bfloat16),
        grid_spec=pltpu.PrefetchScalarGridSpec(
            num_scalar_prefetch=1,
            grid=(NB,),
            in_specs=[pieces, pieces],
            out_specs=pl.BlockSpec((M // NB, 3 * M), lambda b, at: (b, 0)),
        ),
        compiler_params=pltpu.CompilerParams(vmem_limit_bytes=56 * MIB),
        cost_estimate=pl.CostEstimate(
            flops=10_000_000, bytes_accessed=8_000_000, transcendentals=0
        ),
        name="assemble",
    )(place, mine, other)


def lane_index(shape):
    return lax.broadcasted_iota(jnp.int32, shape, len(shape) - 1)


def rolled(x, by):
    by %= 128
    return x if by == 0 else pltpu.roll(x, by, x.ndim - 1)


def pack_kernel(w_ref, p_ref, x_ref, out_ref, stage, tail, in_sems, tail_sems, out_sems):
    fields = (w_ref, p_ref, x_ref)
    last = [
        pltpu.make_async_copy(ref.at[ROWS - 1], tail.at[k], tail_sems.at[k])
        for k, ref in enumerate(fields)
    ]
    fetches = [
        [
            pltpu.make_async_copy(
                ref.at[pl.ds(SHARE * d, SHARE)],
                stage.at[d, pl.ds(SHARE * k, SHARE)],
                in_sems.at[d, k],
            )
            for k, ref in enumerate(fields)
        ]
        for d in range(NB)
    ]
    sends = [
        pltpu.make_async_copy(stage.at[d], out_ref.at[d], out_sems.at[d])
        for d in range(NB)
    ]
    for c in last:
        c.start()
    for group in fetches:
        for c in group:
            c.start()
    for c in last:
        c.wait()
    lane = lane_index((V, 128))
    w, p, x = (tail[k].astype(jnp.float32) for k in range(3))
    for d in range(NB):
        row = jnp.where(lane < 3 * LANES, rolled(x, LANES * (2 - d)), 0.0)
        row = jnp.where(lane < 2 * LANES, rolled(p, LANES * (1 - d)), row)
        row = jnp.where(lane < LANES, rolled(w, LANES * (0 - d)), row)
        stage[d, 3 * SHARE] = row.astype(jnp.bfloat16)
        for c in fetches[d]:
            c.wait()
        sends[d].start()
    for c in sends:
        c.wait()


def pack(w, p, x):
    shape = (NB, 3 * SHARE + 1, V, 128)
    return pl.pallas_call(
        pack_kernel,
        out_shape=jax.ShapeDtypeStruct(shape, jnp.bfloat16),
        in_specs=[ANY] * 3,
        out_specs=ANY,
        scratch_shapes=[
            pltpu.VMEM(shape, jnp.bfloat16),
            pltpu.VMEM((3, V, 128), jnp.bfloat16),
            pltpu.SemaphoreType.DMA((NB, 3)),
            pltpu.SemaphoreType.DMA((3,)),
            pltpu.SemaphoreType.DMA((NB,)),
        ],
        compiler_params=pltpu.CompilerParams(vmem_limit_bytes=56 * MIB),
        cost_estimate=pl.CostEstimate(
            flops=2_000_000, bytes_accessed=12_000_000, transcendentals=0
        ),
        name="pack",
    )(w, p, x)


def rotate_kernel(cells_ref, coef_ref, after_ref, out_ref, cells, out, in_sems, out_sems):
    del after_ref

    def fetch(k, i):
        rows = pl.ds(SHARE * k + 2 * i, 2)
        return pltpu.make_async_copy(
            cells_ref.at[:, rows], cells.at[:, rows], in_sems.at[k, i]
        )

    def put(k, i):
        rows = pl.ds(SHARE * k + 2 * i, 2)
        return pltpu.make_async_copy(
            out.at[:, rows], out_ref.at[:, rows], out_sems.at[k, i]
        )

    steps = SHARE // 2
    fetch_tail = pltpu.make_async_copy(
        cells_ref.at[:, pl.ds(3 * SHARE, 1)],
        cells.at[:, pl.ds(3 * SHARE, 1)],
        in_sems.at[0, steps],
    )
    put_tail = pltpu.make_async_copy(
        out.at[:, pl.ds(2 * SHARE, 1)],
        out_ref.at[:, pl.ds(2 * SHARE, 1)],
        out_sems.at[0, steps],
    )
    for i in range(steps):
        for k in range(3):
            fetch(k, i).start()
    fetch_tail.start()

    def product(w, p, x):
        wp = jnp.concatenate([w, p], axis=0)
        direction = jnp.dot(
            coef_ref[:, M:], wp, preferred_element_type=jnp.float32
        )
        rotated = direction + jnp.dot(
            coef_ref[:, :M], x, preferred_element_type=jnp.float32
        )
        return direction, rotated

    def step(i, carry):
        for k in range(3):
            fetch(k, i).wait()

        def row_pair(k):
            first = cells[:, SHARE * k + 2 * i].reshape(M, 128)
            second = cells[:, SHARE * k + 2 * i + 1].reshape(M, 128)
            return jnp.concatenate([first, second], axis=1)

        results = product(row_pair(0), row_pair(1), row_pair(2))
        for k, result in enumerate(results):
            result = result.astype(jnp.bfloat16)
            for j in range(2):
                part = result[:, 128 * j : 128 * (j + 1)]
                out[:, SHARE * k + 2 * i + j] = part.reshape(NB, V, 128)
            put(k, i).start()
        return carry

    lax.fori_loop(0, steps, step, 0)
    fetch_tail.wait()
    tail = cells[:, 3 * SHARE].reshape(M, 128)
    wide = tail.astype(jnp.float32)
    shifted = [rolled(wide, -LANES * k).astype(jnp.bfloat16) for k in (1, 2)]
    direction, rotated = product(tail, *shifted)
    mixed = jnp.where(
        lane_index((M, 128)) < LANES, direction, rolled(rotated, LANES)
    )
    out[:, 2 * SHARE] = mixed.astype(jnp.bfloat16).reshape(NB, V, 128)
    put_tail.start()
    for k in range(2):
        for i in range(steps):
            put(k, i).wait()
    put_tail.wait()


def rotate(cells, coef, after):
    return pl.pallas_call(
        rotate_kernel,
        out_shape=jax.ShapeDtypeStruct((NB, 2 * SHARE + 1, V, 128), jnp.bfloat16),
        in_specs=[ANY, pl.BlockSpec(memory_space=pltpu.VMEM), ANY],
        out_specs=ANY,
        scratch_shapes=[
            pltpu.VMEM((NB, 3 * SHARE + 1, V, 128), jnp.bfloat16),
            pltpu.VMEM((NB, 2 * SHARE + 1, V, 128), jnp.bfloat16),
            pltpu.SemaphoreType.DMA((3, SHARE // 2 + 1)),
            pltpu.SemaphoreType.DMA((2, SHARE // 2 + 1)),
        ],
        compiler_params=pltpu.CompilerParams(vmem_limit_bytes=24 * MIB),
        cost_estimate=pl.CostEstimate(
            flops=6 * M * M * 128 * (SHARE + 1), bytes_accessed=14_000_000, transcendentals=0
        ),
        name="rotate",
    )(cells, coef, after)


def unpack_kernel(in_ref, d_ref, r_ref, stage, last, in_sems, tail_sems, out_sems, last_sems):
    tails = [
        pltpu.make_async_copy(
            in_ref.at[s, 2 * SHARE], stage.at[s, 2 * SHARE], tail_sems.at[s]
        )
        for s in range(NB)
    ]
    fetches = [
        pltpu.make_async_copy(
            in_ref.at[s, pl.ds(0, 2 * SHARE)],
            stage.at[s, pl.ds(0, 2 * SHARE)],
            in_sems.at[s],
        )
        for s in range(NB)
    ]
    for c in tails + fetches:
        c.start()
    for c in tails:
        c.wait()
    which = lane_index((V, 128)) // LANES
    direction = rotated = jnp.zeros((V, 128), jnp.float32)
    copies = []
    for s in range(NB):
        row = stage[s, 2 * SHARE].astype(jnp.float32)
        direction = jnp.where(which == s, rolled(row, LANES * s), direction)
        rotated = jnp.where(which == s, rolled(row, LANES * (s - 1)), rotated)
        fetches[s].wait()
        for k, ref in enumerate((d_ref, r_ref)):
            copies.append(
                pltpu.make_async_copy(
                    stage.at[s, pl.ds(SHARE * k, SHARE)],
                    ref.at[pl.ds(SHARE * s, SHARE)],
                    out_sems.at[s, k],
                )
            )
            copies[-1].start()
    last[0] = direction.astype(jnp.bfloat16)
    last[1] = rotated.astype(jnp.bfloat16)
    for k, ref in enumerate((d_ref, r_ref)):
        copies.append(pltpu.make_async_copy(last.at[k], ref.at[ROWS - 1], last_sems.at[k]))
        copies[-1].start()
    for c in copies:
        c.wait()


def unpack(parts):
    whole = jax.ShapeDtypeStruct((ROWS, V, 128), jnp.bfloat16)
    return pl.pallas_call(
        unpack_kernel,
        out_shape=(whole, whole),
        in_specs=[ANY],
        out_specs=(ANY, ANY),
        scratch_shapes=[
            pltpu.VMEM((NB, 2 * SHARE + 1, V, 128), jnp.bfloat16),
            pltpu.VMEM((2, V, 128), jnp.bfloat16),
            pltpu.SemaphoreType.DMA((NB,)),
            pltpu.SemaphoreType.DMA((NB,)),
            pltpu.SemaphoreType.DMA((NB, 2)),
            pltpu.SemaphoreType.DMA((2,)),
        ],
        compiler_params=pltpu.CompilerParams(vmem_limit_bytes=8 * MIB),
        name="unpack",
    )(parts)


def hold(arrays, until):
    count = len(arrays)

    def kernel(*refs):
        del refs

    return pl.pallas_call(
        kernel,
        out_shape=[jax.ShapeDtypeStruct(x.shape, x.dtype) for x in arrays],
        in_specs=[ANY] * (count + len(until)),
        out_specs=[ANY] * count,
        input_output_aliases={i: i for i in range(count)},
        name="hold",
    )(*arrays, *until)


NZ, NY = 3, 9
VB = 16


def curl_kernel(
    eps_ref, mat_ref, w_ref, above_ref, below_ref, out_ref, token_ref, tensor, electric
):
    token_ref[...] = jnp.zeros_like(token_ref)

    @pl.when(pl.program_id(0) == 0)
    def _():
        marks = mat_ref[...]
        for c in range(3):
            for d in range(3):
                value = jnp.full(marks.shape, eps_ref[0, c * 3 + d], jnp.float32)
                for m in range(1, NMAT):
                    value = jnp.where(marks == m, eps_ref[m, c * 3 + d], value)
                tensor[c * 3 + d] = 0.25 * value

    def field(c, z, y):
        y %= NY
        if z < 0:
            tile = below_ref[c * NY + y]
        elif z < NZ:
            tile = w_ref[(c * NZ + z) * NY + y]
        else:
            tile = above_ref[c * NY + y]
        return tile.astype(jnp.float32)

    for z in range(-1, NZ):
        for y in range(NY):
            hx, hy, hz = (field(c, z, y) for c in range(3))
            curl = (
                (field(2, z, y + 1) - hz) - (field(1, z + 1, y) - hy),
                (field(0, z + 1, y) - hx) - (rolled(hz, -1) - hz),
                (rolled(hy, -1) - hy) - (field(0, z, y + 1) - hx),
            )
            for c in range(3 if z >= 0 else 2):
                total = None
                for d in range(3):
                    weight = tensor[c * 3 + d, pl.ds((z + 1) * NY + y, 1)]
                    term = weight * curl[d]
                    total = term if total is None else total + term
                electric[c, (z + 1) * NY + y] = total
    for z in range(NZ):
        for y in range(NY):
            before = (y - 1) % NY
            here = (z + 1) * NY
            ex, ey, ez = (electric[c, here + y] for c in range(3))
            applied = (
                (ez - electric[2, here + before]) - (ey - electric[1, here + y - NY]),
                (ex - electric[0, here + y - NY]) - (ez - rolled(ez, 1)),
                (ey - rolled(ey, 1)) - (ex - electric[0, here + before]),
            )
            for c in range(3):
                out_ref[(c * NZ + z) * NY + y] = applied[c].astype(jnp.bfloat16)


def apply_curls(w, above, below, marks, eps):
    block = lambda rows: pl.BlockSpec((rows, VB, 128), lambda i: (0, i, 0))
    return pl.pallas_call(
        curl_kernel,
        out_shape=(
            jax.ShapeDtypeStruct((ROWS, V, 128), jnp.bfloat16),
            jax.ShapeDtypeStruct((8, 128), jnp.float32),
        ),
        grid=(V // VB,),
        in_specs=[
            pl.BlockSpec(memory_space=pltpu.SMEM),
            pl.BlockSpec(memory_space=pltpu.VMEM),
            block(ROWS),
            block(2 * NY),
            block(3 * NY),
        ],
        out_specs=(block(ROWS), pl.BlockSpec((8, 128), lambda i: (0, 0))),
        scratch_shapes=[
            pltpu.VMEM((9, (NZ + 1) * NY, 128), jnp.float32),
            pltpu.VMEM((3, (NZ + 1) * NY, VB, 128), jnp.float32),
        ],
        compiler_params=pltpu.CompilerParams(vmem_limit_bytes=56 * MIB),
        cost_estimate=pl.CostEstimate(
            flops=60_000_000, bytes_accessed=5_000_000, transcendentals=0
        ),
        name="curls",
    )(eps, marks, w, above, below)


def as_rows(x):
    return x.transpose(1, 2, 3, 0, 4).reshape(ROWS, V, 128)


def as_block(rows):
    return rows.reshape(3, NZ, NY, V, 128).transpose(3, 0, 1, 2, 4)


def per_device(current, search, previous, coefficients, material, inverse_permittivity):
    w, p, x = as_rows(search), as_rows(previous), as_rows(current)
    slab, blk = lax.axis_index("slab"), lax.axis_index("blk")
    place = jnp.stack([slab // 16, (slab // 2) % 8, slab % 2, blk // 2, blk % 2])
    mark_below = ring_shift(material[NZ - 1 :], "slab", 1)
    marks = jnp.concatenate([mark_below, material]).reshape((NZ + 1) * NY, 128)
    packed = pack(w, p, x)
    plane = gather_plane(coefficients)
    packed, plane = lax.optimization_barrier((packed, plane))
    cells = lax.all_to_all(packed, "blk", split_axis=0, concat_axis=0, tiled=True)
    groups = [[h * 16 + z * 2 + c for z in range(8)] for h in range(2) for c in range(2)]
    mine = lax.all_gather(plane, "slab", axis_index_groups=groups)
    other = move(mine, "slab", SLAB, (0, 0, 1))
    coef = assemble(place, mine, other)
    layers = w.reshape(3, NZ, NY, V, 128)
    low = layers[:2, 0].reshape(2 * NY, V, 128)
    high = layers[:, NZ - 1].reshape(3 * NY, V, 128)
    low, high = hold([low, high], [mine])
    above = ring_shift(low, "slab", -1)
    below = ring_shift(high, "slab", 1)
    applied, token = apply_curls(w, above, below, marks, inverse_permittivity.reshape(NMAT, 9))
    parts = rotate(cells, coef, token)
    back = lax.all_to_all(parts, "blk", split_axis=0, concat_axis=0, tiled=True)
    direction, rotated = unpack(back)
    return as_block(applied), as_block(rotated), as_block(direction)


def solution(mesh):
    block = P("blk", None, "slab", None, None)
    return jax.shard_map(
        per_device,
        mesh=mesh,
        in_specs=(block, block, block, P("slab", "blk"), P("slab", None, None), P()),
        out_specs=(block, block, block),
        check_vma=False,
    )
```

```python
import functools
import itertools

import jax
import jax.numpy as jnp
from jax import lax
from jax.experimental import pallas as pl
from jax.experimental.pallas import tpu as pltpu
from jax.sharding import PartitionSpec as P

M = 768
NMAT = 4
V = 96
NB = 8
ROWS = 81
SHARE = 10
LANES = 128 // NB
SLAB = (2, 8, 2)
BLK = (4, 2)
ANY = pl.BlockSpec(memory_space=pl.ANY)
MIB = 1024 * 1024


def move(x, axis, sizes, steps):
    pairs = []
    for place in itertools.product(*[range(n) for n in sizes]):
        src = dst = 0
        for n, p, s in zip(sizes, place, steps):
            src = src * n + p
            dst = dst * n + (p + s) % n
        pairs.append((src, dst))
    return lax.ppermute(x, axis, pairs)


def ring_shift(x, axis, by):
    count = lax.axis_size(axis)
    return lax.ppermute(x, axis, [(i, (i + by) % count) for i in range(count)])


def gather_plane(tile):
    pieces = [tile]
    pieces.append(move(tile, "blk", BLK, (0, 1)))
    pieces.append(move(tile, "slab", SLAB, (1, 0, 0)))
    pieces.append(
        lax.ppermute(
            tile,
            ("slab", "blk"),
            [
                (s * NB + b, (s + 16) % 32 * NB + (b ^ 1))
                for s in range(32)
                for b in range(NB)
            ],
        )
    )
    t = jnp.stack(pieces)
    plane = jnp.stack([t] + [move(t, "blk", BLK, (-k, 0)) for k in (1, 2, 3)])
    return plane, pieces[1:]


def assemble_kernel(place_ref, mine_ref, other_ref, out_ref):
    here, core = place_ref[0], place_ref[2]
    tiles = []
    for y_hi in range(2):
        k = (y_hi - here + 2) % 2
        for z in range(8):
            own = mine_ref[z, 0, k, 0].astype(jnp.float32)
            far = other_ref[z, 0, k, 0].astype(jnp.float32)
            tiles.append(jnp.where(core == 0, own, far))
            tiles.append(jnp.where(core == 0, far, own))
    out_ref[...] = jnp.concatenate(tiles, axis=0).T.astype(jnp.bfloat16)


def assemble(place, mine, other):
    def piece(b, at):
        return 0, (b // 2 - at[3] + 4) % 4, 0, (b % 2 - at[4] + 2) % 2, 0, 0

    mine, other = (t.reshape(8, 4, 2, 2, 72, 96) for t in (mine, other))
    pieces = pl.BlockSpec((8, 1, 2, 1, 72, 96), piece)
    return pl.pallas_call(
        assemble_kernel,
        out_shape=jax.ShapeDtypeStruct((M, 3 * M), jnp.bfloat16),
        grid_spec=pltpu.PrefetchScalarGridSpec(
            num_scalar_prefetch=1,
            grid=(NB,),
            in_specs=[pieces, pieces],
            out_specs=pl.BlockSpec((M // NB, 3 * M), lambda b, at: (b, 0)),
        ),
        compiler_params=pltpu.CompilerParams(vmem_limit_bytes=56 * MIB),
        cost_estimate=pl.CostEstimate(
            flops=10_000_000, bytes_accessed=8_000_000, transcendentals=0
        ),
        name="assemble",
    )(place, mine, other)


def lane_index(shape):
    return lax.broadcasted_iota(jnp.int32, shape, len(shape) - 1)


def rolled(x, by):
    by %= 128
    return x if by == 0 else pltpu.roll(x, by, x.ndim - 1)


def pack_kernel(w_ref, p_ref, x_ref, out_ref, stage, tail, in_sems, tail_sems, out_sems):
    fields = (w_ref, p_ref, x_ref)
    last = [
        pltpu.make_async_copy(ref.at[ROWS - 1], tail.at[k], tail_sems.at[k])
        for k, ref in enumerate(fields)
    ]
    fetches = [
        [
            pltpu.make_async_copy(
                ref.at[pl.ds(SHARE * d, SHARE)],
                stage.at[d, pl.ds(SHARE * k, SHARE)],
                in_sems.at[d, k],
            )
            for k, ref in enumerate(fields)
        ]
        for d in range(NB)
    ]
    sends = [
        pltpu.make_async_copy(stage.at[d], out_ref.at[d], out_sems.at[d])
        for d in range(NB)
    ]
    for c in last:
        c.start()
    for group in fetches:
        for c in group:
            c.start()
    for c in last:
        c.wait()
    lane = lane_index((V, 128))
    w, p, x = (tail[k].astype(jnp.float32) for k in range(3))
    for d in range(NB):
        row = jnp.where(lane < 3 * LANES, rolled(x, LANES * (2 - d)), 0.0)
        row = jnp.where(lane < 2 * LANES, rolled(p, LANES * (1 - d)), row)
        row = jnp.where(lane < LANES, rolled(w, LANES * (0 - d)), row)
        stage[d, 3 * SHARE] = row.astype(jnp.bfloat16)
        for c in fetches[d]:
            c.wait()
        sends[d].start()
    for c in sends:
        c.wait()


def pack(w, p, x):
    shape = (NB, 3 * SHARE + 1, V, 128)
    return pl.pallas_call(
        pack_kernel,
        out_shape=jax.ShapeDtypeStruct(shape, jnp.bfloat16),
        in_specs=[ANY] * 3,
        out_specs=ANY,
        scratch_shapes=[
            pltpu.VMEM(shape, jnp.bfloat16),
            pltpu.VMEM((3, V, 128), jnp.bfloat16),
            pltpu.SemaphoreType.DMA((NB, 3)),
            pltpu.SemaphoreType.DMA((3,)),
            pltpu.SemaphoreType.DMA((NB,)),
        ],
        compiler_params=pltpu.CompilerParams(vmem_limit_bytes=56 * MIB),
        cost_estimate=pl.CostEstimate(
            flops=2_000_000, bytes_accessed=12_000_000, transcendentals=0
        ),
        name="pack",
    )(w, p, x)


def rotate_kernel(cells_ref, coef_ref, after_ref, out_ref, cells, out, in_sems, out_sems):
    del after_ref

    def fetch(k, i):
        rows = pl.ds(SHARE * k + 2 * i, 2)
        return pltpu.make_async_copy(
            cells_ref.at[:, rows], cells.at[:, rows], in_sems.at[k, i]
        )

    def put(k, i):
        rows = pl.ds(SHARE * k + 2 * i, 2)
        return pltpu.make_async_copy(
            out.at[:, rows], out_ref.at[:, rows], out_sems.at[k, i]
        )

    steps = SHARE // 2
    fetch_tail = pltpu.make_async_copy(
        cells_ref.at[:, pl.ds(3 * SHARE, 1)],
        cells.at[:, pl.ds(3 * SHARE, 1)],
        in_sems.at[0, steps],
    )
    put_tail = pltpu.make_async_copy(
        out.at[:, pl.ds(2 * SHARE, 1)],
        out_ref.at[:, pl.ds(2 * SHARE, 1)],
        out_sems.at[0, steps],
    )
    for i in range(steps):
        for k in range(3):
            fetch(k, i).start()
    fetch_tail.start()

    def product(w, p, x):
        wp = jnp.concatenate([w, p], axis=0)
        direction = jnp.dot(
            coef_ref[:, M:], wp, preferred_element_type=jnp.float32
        )
        rotated = direction + jnp.dot(
            coef_ref[:, :M], x, preferred_element_type=jnp.float32
        )
        return direction, rotated

    def step(i, carry):
        for k in range(3):
            fetch(k, i).wait()

        def row_pair(k):
            first = cells[:, SHARE * k + 2 * i].reshape(M, 128)
            second = cells[:, SHARE * k + 2 * i + 1].reshape(M, 128)
            return jnp.concatenate([first, second], axis=1)

        results = product(row_pair(0), row_pair(1), row_pair(2))
        for k, result in enumerate(results):
            result = result.astype(jnp.bfloat16)
            for j in range(2):
                part = result[:, 128 * j : 128 * (j + 1)]
                out[:, SHARE * k + 2 * i + j] = part.reshape(NB, V, 128)
            put(k, i).start()
        return carry

    lax.fori_loop(0, steps, step, 0)
    fetch_tail.wait()
    tail = cells[:, 3 * SHARE].reshape(M, 128)
    wide = tail.astype(jnp.float32)
    shifted = [rolled(wide, -LANES * k).astype(jnp.bfloat16) for k in (1, 2)]
    direction, rotated = product(tail, *shifted)
    mixed = jnp.where(
        lane_index((M, 128)) < LANES, direction, rolled(rotated, LANES)
    )
    out[:, 2 * SHARE] = mixed.astype(jnp.bfloat16).reshape(NB, V, 128)
    put_tail.start()
    for k in range(2):
        for i in range(steps):
            put(k, i).wait()
    put_tail.wait()


def rotate(cells, coef, after):
    return pl.pallas_call(
        rotate_kernel,
        out_shape=jax.ShapeDtypeStruct((NB, 2 * SHARE + 1, V, 128), jnp.bfloat16),
        in_specs=[ANY, pl.BlockSpec(memory_space=pltpu.VMEM), ANY],
        out_specs=ANY,
        scratch_shapes=[
            pltpu.VMEM((NB, 3 * SHARE + 1, V, 128), jnp.bfloat16),
            pltpu.VMEM((NB, 2 * SHARE + 1, V, 128), jnp.bfloat16),
            pltpu.SemaphoreType.DMA((3, SHARE // 2 + 1)),
            pltpu.SemaphoreType.DMA((2, SHARE // 2 + 1)),
        ],
        compiler_params=pltpu.CompilerParams(vmem_limit_bytes=24 * MIB),
        cost_estimate=pl.CostEstimate(
            flops=6 * M * M * 128 * (SHARE + 1), bytes_accessed=14_000_000, transcendentals=0
        ),
        name="rotate",
    )(cells, coef, after)


def unpack_kernel(parts, d_ref, r_ref, last, out_sems, last_sems):
    copies = []
    for s in range(NB):
        for k, ref in enumerate((d_ref, r_ref)):
            copies.append(
                pltpu.make_async_copy(
                    parts.at[s, pl.ds(SHARE * k, SHARE)],
                    ref.at[pl.ds(SHARE * s, SHARE)],
                    out_sems.at[s, k],
                )
            )
            copies[-1].start()
    which = lane_index((V, 128)) // LANES
    direction = rotated = jnp.zeros((V, 128), jnp.float32)
    for s in range(NB):
        row = parts[s, 2 * SHARE].astype(jnp.float32)
        direction = jnp.where(which == s, rolled(row, LANES * s), direction)
        rotated = jnp.where(which == s, rolled(row, LANES * (s - 1)), rotated)
    last[0] = direction.astype(jnp.bfloat16)
    last[1] = rotated.astype(jnp.bfloat16)
    for k, ref in enumerate((d_ref, r_ref)):
        copies.append(pltpu.make_async_copy(last.at[k], ref.at[ROWS - 1], last_sems.at[k]))
        copies[-1].start()
    for c in copies:
        c.wait()


def unpack(parts):
    whole = jax.ShapeDtypeStruct((ROWS, V, 128), jnp.bfloat16)
    return pl.pallas_call(
        unpack_kernel,
        out_shape=(whole, whole),
        in_specs=[pl.BlockSpec(memory_space=pltpu.VMEM)],
        out_specs=(ANY, ANY),
        scratch_shapes=[
            pltpu.VMEM((2, V, 128), jnp.bfloat16),
            pltpu.SemaphoreType.DMA((NB, 2)),
            pltpu.SemaphoreType.DMA((2,)),
        ],
        compiler_params=pltpu.CompilerParams(vmem_limit_bytes=12 * MIB),
        name="unpack",
    )(parts)


def hold(arrays, until):
    count = len(arrays)

    def kernel(*refs):
        del refs

    return pl.pallas_call(
        kernel,
        out_shape=[jax.ShapeDtypeStruct(x.shape, x.dtype) for x in arrays],
        in_specs=[ANY] * (count + len(until)),
        out_specs=[ANY] * count,
        input_output_aliases={i: i for i in range(count)},
        name="hold",
    )(*arrays, *until)


NZ, NY = 3, 9
VB = 16


def curl_kernel(
    eps_ref, mat_ref, w_ref, above_ref, below_ref, out_ref, token_ref, tensor, electric
):
    token_ref[...] = jnp.zeros_like(token_ref)

    @pl.when(pl.program_id(0) == 0)
    def _():
        marks = mat_ref[...]
        for c in range(3):
            for d in range(3):
                value = jnp.full(marks.shape, eps_ref[0, c * 3 + d], jnp.float32)
                for m in range(1, NMAT):
                    value = jnp.where(marks == m, eps_ref[m, c * 3 + d], value)
                tensor[c * 3 + d] = 0.25 * value

    def field(c, z, y):
        y %= NY
        if z < 0:
            tile = below_ref[c * NY + y]
        elif z < NZ:
            tile = w_ref[(c * NZ + z) * NY + y]
        else:
            tile = above_ref[c * NY + y]
        return tile.astype(jnp.float32)

    for z in range(-1, NZ):
        for y in range(NY):
            hx, hy, hz = (field(c, z, y) for c in range(3))
            curl = (
                (field(2, z, y + 1) - hz) - (field(1, z + 1, y) - hy),
                (field(0, z + 1, y) - hx) - (rolled(hz, -1) - hz),
                (rolled(hy, -1) - hy) - (field(0, z, y + 1) - hx),
            )
            for c in range(3 if z >= 0 else 2):
                total = None
                for d in range(3):
                    weight = tensor[c * 3 + d, pl.ds((z + 1) * NY + y, 1)]
                    term = weight * curl[d]
                    total = term if total is None else total + term
                electric[c, (z + 1) * NY + y] = total
    for z in range(NZ):
        for y in range(NY):
            before = (y - 1) % NY
            here = (z + 1) * NY
            ex, ey, ez = (electric[c, here + y] for c in range(3))
            applied = (
                (ez - electric[2, here + before]) - (ey - electric[1, here + y - NY]),
                (ex - electric[0, here + y - NY]) - (ez - rolled(ez, 1)),
                (ey - rolled(ey, 1)) - (ex - electric[0, here + before]),
            )
            for c in range(3):
                out_ref[(c * NZ + z) * NY + y] = applied[c].astype(jnp.bfloat16)


def apply_curls(w, above, below, marks, eps):
    block = lambda rows: pl.BlockSpec((rows, VB, 128), lambda i: (0, i, 0))
    return pl.pallas_call(
        curl_kernel,
        out_shape=(
            jax.ShapeDtypeStruct((ROWS, V, 128), jnp.bfloat16),
            jax.ShapeDtypeStruct((8, 128), jnp.float32),
        ),
        grid=(V // VB,),
        in_specs=[
            pl.BlockSpec(memory_space=pltpu.SMEM),
            pl.BlockSpec(memory_space=pltpu.VMEM),
            block(ROWS),
            block(2 * NY),
            block(3 * NY),
        ],
        out_specs=(block(ROWS), pl.BlockSpec((8, 128), lambda i: (0, 0))),
        scratch_shapes=[
            pltpu.VMEM((9, (NZ + 1) * NY, 128), jnp.float32),
            pltpu.VMEM((3, (NZ + 1) * NY, VB, 128), jnp.float32),
        ],
        compiler_params=pltpu.CompilerParams(vmem_limit_bytes=56 * MIB),
        cost_estimate=pl.CostEstimate(
            flops=60_000_000, bytes_accessed=5_000_000, transcendentals=0
        ),
        name="curls",
    )(eps, marks, w, above, below)


def as_rows(x):
    return x.transpose(1, 2, 3, 0, 4).reshape(ROWS, V, 128)


def as_block(rows):
    return rows.reshape(3, NZ, NY, V, 128).transpose(3, 0, 1, 2, 4)


def per_device(current, search, previous, coefficients, material, inverse_permittivity):
    w, p, x = as_rows(search), as_rows(previous), as_rows(current)
    slab, blk = lax.axis_index("slab"), lax.axis_index("blk")
    place = jnp.stack([slab // 16, (slab // 2) % 8, slab % 2, blk // 2, blk % 2])
    plane, first = gather_plane(coefficients)
    layers = w.reshape(3, NZ, NY, V, 128)
    low = layers[:2, 0].reshape(2 * NY, V, 128)
    high = layers[:, NZ - 1].reshape(3 * NY, V, 128)
    low, high = hold([low, high], first)
    below = ring_shift(high, "slab", 1)
    above = ring_shift(low, "slab", -1)
    packed = pack(w, p, x)
    packed, plane = lax.optimization_barrier((packed, plane))
    (packed,) = hold([packed], [below, above])
    cells = lax.all_to_all(packed, "blk", split_axis=0, concat_axis=0, tiled=True)
    groups = [[h * 16 + z * 2 + c for z in range(8)] for h in range(2) for c in range(2)]
    mine = lax.all_gather(plane, "slab", axis_index_groups=groups)
    other = move(mine, "slab", SLAB, (0, 0, 1))
    coef = assemble(place, mine, other)
    mark_below = ring_shift(material[NZ - 1 :], "slab", 1)
    marks = jnp.concatenate([mark_below, material]).reshape((NZ + 1) * NY, 128)
    applied, token = apply_curls(w, above, below, marks, inverse_permittivity.reshape(NMAT, 9))
    parts = rotate(cells, coef, token)
    back = lax.all_to_all(parts, "blk", split_axis=0, concat_axis=0, tiled=True)
    direction, rotated = unpack(back)
    return as_block(applied), as_block(rotated), as_block(direction)


def solution(mesh):
    block = P("blk", None, "slab", None, None)
    return jax.shard_map(
        per_device,
        mesh=mesh,
        in_specs=(block, block, block, P("slab", "blk"), P("slab", None, None), P()),
        out_specs=(block, block, block),
        check_vma=False,
    )
```

```python
import functools
import itertools

import jax
import jax.numpy as jnp
from jax import lax
from jax.experimental import pallas as pl
from jax.experimental.pallas import tpu as pltpu
from jax.sharding import PartitionSpec as P

M = 768
NMAT = 4
V = 96
NB = 8
ROWS = 81
SHARE = 10
LANES = 128 // NB
SLAB = (2, 8, 2)
BLK = (4, 2)
ANY = pl.BlockSpec(memory_space=pl.ANY)
MIB = 1024 * 1024


def move(x, axis, sizes, steps):
    pairs = []
    for place in itertools.product(*[range(n) for n in sizes]):
        src = dst = 0
        for n, p, s in zip(sizes, place, steps):
            src = src * n + p
            dst = dst * n + (p + s) % n
        pairs.append((src, dst))
    return lax.ppermute(x, axis, pairs)


def ring_shift(x, axis, by):
    count = lax.axis_size(axis)
    return lax.ppermute(x, axis, [(i, (i + by) % count) for i in range(count)])


def gather_plane(tile):
    pieces = [tile]
    pieces.append(move(tile, "blk", BLK, (0, 1)))
    pieces.append(move(tile, "slab", SLAB, (1, 0, 0)))
    pieces.append(
        lax.ppermute(
            tile,
            ("slab", "blk"),
            [
                (s * NB + b, (s + 16) % 32 * NB + (b ^ 1))
                for s in range(32)
                for b in range(NB)
            ],
        )
    )
    t = jnp.stack(pieces)
    return jnp.stack([t] + [move(t, "blk", BLK, (-k, 0)) for k in (1, 2, 3)])


def assemble_kernel(place_ref, mine_ref, other_ref, out_ref):
    here, core = place_ref[0], place_ref[2]
    tiles = []
    for y_hi in range(2):
        k = (y_hi - here + 2) % 2
        for z in range(8):
            own = mine_ref[z, 0, k, 0].astype(jnp.float32)
            far = other_ref[z, 0, k, 0].astype(jnp.float32)
            tiles.append(jnp.where(core == 0, own, far))
            tiles.append(jnp.where(core == 0, far, own))
    out_ref[...] = jnp.concatenate(tiles, axis=0).T.astype(jnp.bfloat16)


def assemble(place, mine, other):
    def piece(b, at):
        return 0, (b // 2 - at[3] + 4) % 4, 0, (b % 2 - at[4] + 2) % 2, 0, 0

    mine, other = (t.reshape(8, 4, 2, 2, 72, 96) for t in (mine, other))
    pieces = pl.BlockSpec((8, 1, 2, 1, 72, 96), piece)
    return pl.pallas_call(
        assemble_kernel,
        out_shape=jax.ShapeDtypeStruct((M, 3 * M), jnp.bfloat16),
        grid_spec=pltpu.PrefetchScalarGridSpec(
            num_scalar_prefetch=1,
            grid=(NB,),
            in_specs=[pieces, pieces],
            out_specs=pl.BlockSpec((M // NB, 3 * M), lambda b, at: (b, 0)),
        ),
        compiler_params=pltpu.CompilerParams(vmem_limit_bytes=56 * MIB),
        cost_estimate=pl.CostEstimate(
            flops=10_000_000, bytes_accessed=8_000_000, transcendentals=0
        ),
        name="assemble",
    )(place, mine, other)


def lane_index(shape):
    return lax.broadcasted_iota(jnp.int32, shape, len(shape) - 1)


def rolled(x, by):
    by %= 128
    return x if by == 0 else pltpu.roll(x, by, x.ndim - 1)


def pack_kernel(w_ref, p_ref, x_ref, out_ref, stage, tail, in_sems, tail_sems, out_sems):
    fields = (w_ref, p_ref, x_ref)
    last = [
        pltpu.make_async_copy(ref.at[ROWS - 1], tail.at[k], tail_sems.at[k])
        for k, ref in enumerate(fields)
    ]
    fetches = [
        [
            pltpu.make_async_copy(
                ref.at[pl.ds(SHARE * d, SHARE)],
                stage.at[d, pl.ds(SHARE * k, SHARE)],
                in_sems.at[d, k],
            )
            for k, ref in enumerate(fields)
        ]
        for d in range(NB)
    ]
    sends = [
        pltpu.make_async_copy(stage.at[d], out_ref.at[d], out_sems.at[d])
        for d in range(NB)
    ]
    for c in last:
        c.start()
    for group in fetches:
        for c in group:
            c.start()
    for c in last:
        c.wait()
    lane = lane_index((V, 128))
    w, p, x = (tail[k].astype(jnp.float32) for k in range(3))
    for d in range(NB):
        row = jnp.where(lane < 3 * LANES, rolled(x, LANES * (2 - d)), 0.0)
        row = jnp.where(lane < 2 * LANES, rolled(p, LANES * (1 - d)), row)
        row = jnp.where(lane < LANES, rolled(w, LANES * (0 - d)), row)
        stage[d, 3 * SHARE] = row.astype(jnp.bfloat16)
        for c in fetches[d]:
            c.wait()
        sends[d].start()
    for c in sends:
        c.wait()


def pack(w, p, x):
    shape = (NB, 3 * SHARE + 1, V, 128)
    return pl.pallas_call(
        pack_kernel,
        out_shape=jax.ShapeDtypeStruct(shape, jnp.bfloat16),
        in_specs=[ANY] * 3,
        out_specs=ANY,
        scratch_shapes=[
            pltpu.VMEM(shape, jnp.bfloat16),
            pltpu.VMEM((3, V, 128), jnp.bfloat16),
            pltpu.SemaphoreType.DMA((NB, 3)),
            pltpu.SemaphoreType.DMA((3,)),
            pltpu.SemaphoreType.DMA((NB,)),
        ],
        compiler_params=pltpu.CompilerParams(vmem_limit_bytes=56 * MIB),
        cost_estimate=pl.CostEstimate(
            flops=2_000_000, bytes_accessed=12_000_000, transcendentals=0
        ),
        name="pack",
    )(w, p, x)


def rotate_kernel(cells_ref, coef_ref, after_ref, out_ref, cells, out, in_sems, out_sems):
    del after_ref

    def fetch(k, i):
        rows = pl.ds(SHARE * k + 2 * i, 2)
        return pltpu.make_async_copy(
            cells_ref.at[:, rows], cells.at[:, rows], in_sems.at[k, i]
        )

    def put(k, i):
        rows = pl.ds(SHARE * k + 2 * i, 2)
        return pltpu.make_async_copy(
            out.at[:, rows], out_ref.at[:, rows], out_sems.at[k, i]
        )

    steps = SHARE // 2
    fetch_tail = pltpu.make_async_copy(
        cells_ref.at[:, pl.ds(3 * SHARE, 1)],
        cells.at[:, pl.ds(3 * SHARE, 1)],
        in_sems.at[0, steps],
    )
    put_tail = pltpu.make_async_copy(
        out.at[:, pl.ds(2 * SHARE, 1)],
        out_ref.at[:, pl.ds(2 * SHARE, 1)],
        out_sems.at[0, steps],
    )
    for i in range(steps):
        for k in range(3):
            fetch(k, i).start()
    fetch_tail.start()

    def product(w, p, x):
        wp = jnp.concatenate([w, p], axis=0)
        direction = jnp.dot(
            coef_ref[:, M:], wp, preferred_element_type=jnp.float32
        )
        rotated = direction + jnp.dot(
            coef_ref[:, :M], x, preferred_element_type=jnp.float32
        )
        return direction, rotated

    def step(i, carry):
        for k in range(3):
            fetch(k, i).wait()

        def row_pair(k):
            first = cells[:, SHARE * k + 2 * i].reshape(M, 128)
            second = cells[:, SHARE * k + 2 * i + 1].reshape(M, 128)
            return jnp.concatenate([first, second], axis=1)

        results = product(row_pair(0), row_pair(1), row_pair(2))
        for k, result in enumerate(results):
            result = result.astype(jnp.bfloat16)
            for j in range(2):
                part = result[:, 128 * j : 128 * (j + 1)]
                out[:, SHARE * k + 2 * i + j] = part.reshape(NB, V, 128)
            put(k, i).start()
        return carry

    lax.fori_loop(0, steps, step, 0)
    fetch_tail.wait()
    tail = cells[:, 3 * SHARE].reshape(M, 128)
    wide = tail.astype(jnp.float32)
    shifted = [rolled(wide, -LANES * k).astype(jnp.bfloat16) for k in (1, 2)]
    direction, rotated = product(tail, *shifted)
    mixed = jnp.where(
        lane_index((M, 128)) < LANES, direction, rolled(rotated, LANES)
    )
    out[:, 2 * SHARE] = mixed.astype(jnp.bfloat16).reshape(NB, V, 128)
    put_tail.start()
    for k in range(2):
        for i in range(steps):
            put(k, i).wait()
    put_tail.wait()


def rotate(cells, coef, after):
    return pl.pallas_call(
        rotate_kernel,
        out_shape=jax.ShapeDtypeStruct((NB, 2 * SHARE + 1, V, 128), jnp.bfloat16),
        in_specs=[ANY, pl.BlockSpec(memory_space=pltpu.VMEM), ANY],
        out_specs=ANY,
        scratch_shapes=[
            pltpu.VMEM((NB, 3 * SHARE + 1, V, 128), jnp.bfloat16),
            pltpu.VMEM((NB, 2 * SHARE + 1, V, 128), jnp.bfloat16),
            pltpu.SemaphoreType.DMA((3, SHARE // 2 + 1)),
            pltpu.SemaphoreType.DMA((2, SHARE // 2 + 1)),
        ],
        compiler_params=pltpu.CompilerParams(vmem_limit_bytes=24 * MIB),
        cost_estimate=pl.CostEstimate(
            flops=6 * M * M * 128 * (SHARE + 1), bytes_accessed=14_000_000, transcendentals=0
        ),
        name="rotate",
    )(cells, coef, after)


def unpack_kernel(parts, d_ref, r_ref, last, out_sems, last_sems):
    copies = []
    for s in range(NB):
        for k, ref in enumerate((d_ref, r_ref)):
            copies.append(
                pltpu.make_async_copy(
                    parts.at[s, pl.ds(SHARE * k, SHARE)],
                    ref.at[pl.ds(SHARE * s, SHARE)],
                    out_sems.at[s, k],
                )
            )
            copies[-1].start()
    which = lane_index((V, 128)) // LANES
    direction = rotated = jnp.zeros((V, 128), jnp.float32)
    for s in range(NB):
        row = parts[s, 2 * SHARE].astype(jnp.float32)
        direction = jnp.where(which == s, rolled(row, LANES * s), direction)
        rotated = jnp.where(which == s, rolled(row, LANES * (s - 1)), rotated)
    last[0] = direction.astype(jnp.bfloat16)
    last[1] = rotated.astype(jnp.bfloat16)
    for k, ref in enumerate((d_ref, r_ref)):
        copies.append(pltpu.make_async_copy(last.at[k], ref.at[ROWS - 1], last_sems.at[k]))
        copies[-1].start()
    for c in copies:
        c.wait()


def unpack(parts):
    whole = jax.ShapeDtypeStruct((ROWS, V, 128), jnp.bfloat16)
    return pl.pallas_call(
        unpack_kernel,
        out_shape=(whole, whole),
        in_specs=[pl.BlockSpec(memory_space=pltpu.VMEM)],
        out_specs=(ANY, ANY),
        scratch_shapes=[
            pltpu.VMEM((2, V, 128), jnp.bfloat16),
            pltpu.SemaphoreType.DMA((NB, 2)),
            pltpu.SemaphoreType.DMA((2,)),
        ],
        compiler_params=pltpu.CompilerParams(vmem_limit_bytes=12 * MIB),
        name="unpack",
    )(parts)


def hold(arrays, until):
    count = len(arrays)

    def kernel(*refs):
        del refs

    return pl.pallas_call(
        kernel,
        out_shape=[jax.ShapeDtypeStruct(x.shape, x.dtype) for x in arrays],
        in_specs=[ANY] * (count + len(until)),
        out_specs=[ANY] * count,
        input_output_aliases={i: i for i in range(count)},
        name="hold",
    )(*arrays, *until)


NZ, NY = 3, 9
VB = 16


def curl_kernel(
    eps_ref, mat_ref, w_ref, above_ref, below_ref, out_ref, token_ref, tensor, electric
):
    token_ref[...] = jnp.zeros_like(token_ref)

    @pl.when(pl.program_id(0) == 0)
    def _():
        marks = mat_ref[...]
        for c in range(3):
            for d in range(3):
                value = jnp.full(marks.shape, eps_ref[0, c * 3 + d], jnp.float32)
                for m in range(1, NMAT):
                    value = jnp.where(marks == m, eps_ref[m, c * 3 + d], value)
                tensor[c * 3 + d] = 0.25 * value

    def field(c, z, y):
        y %= NY
        if z < 0:
            tile = below_ref[c * NY + y]
        elif z < NZ:
            tile = w_ref[(c * NZ + z) * NY + y]
        else:
            tile = above_ref[c * NY + y]
        return tile.astype(jnp.float32)

    for z in range(-1, NZ):
        for y in range(NY):
            hx, hy, hz = (field(c, z, y) for c in range(3))
            curl = (
                (field(2, z, y + 1) - hz) - (field(1, z + 1, y) - hy),
                (field(0, z + 1, y) - hx) - (rolled(hz, -1) - hz),
                (rolled(hy, -1) - hy) - (field(0, z, y + 1) - hx),
            )
            for c in range(3 if z >= 0 else 2):
                total = None
                for d in range(3):
                    weight = tensor[c * 3 + d, pl.ds((z + 1) * NY + y, 1)]
                    term = weight * curl[d]
                    total = term if total is None else total + term
                electric[c, (z + 1) * NY + y] = total
    for z in range(NZ):
        for y in range(NY):
            before = (y - 1) % NY
            here = (z + 1) * NY
            ex, ey, ez = (electric[c, here + y] for c in range(3))
            applied = (
                (ez - electric[2, here + before]) - (ey - electric[1, here + y - NY]),
                (ex - electric[0, here + y - NY]) - (ez - rolled(ez, 1)),
                (ey - rolled(ey, 1)) - (ex - electric[0, here + before]),
            )
            for c in range(3):
                out_ref[(c * NZ + z) * NY + y] = applied[c].astype(jnp.bfloat16)


def apply_curls(w, above, below, marks, eps):
    block = lambda rows: pl.BlockSpec((rows, VB, 128), lambda i: (0, i, 0))
    return pl.pallas_call(
        curl_kernel,
        out_shape=(
            jax.ShapeDtypeStruct((ROWS, V, 128), jnp.bfloat16),
            jax.ShapeDtypeStruct((8, 128), jnp.float32),
        ),
        grid=(V // VB,),
        in_specs=[
            pl.BlockSpec(memory_space=pltpu.SMEM),
            pl.BlockSpec(memory_space=pltpu.VMEM),
            block(ROWS),
            block(2 * NY),
            block(3 * NY),
        ],
        out_specs=(block(ROWS), pl.BlockSpec((8, 128), lambda i: (0, 0))),
        scratch_shapes=[
            pltpu.VMEM((9, (NZ + 1) * NY, 128), jnp.float32),
            pltpu.VMEM((3, (NZ + 1) * NY, VB, 128), jnp.float32),
        ],
        compiler_params=pltpu.CompilerParams(vmem_limit_bytes=56 * MIB),
        cost_estimate=pl.CostEstimate(
            flops=60_000_000, bytes_accessed=5_000_000, transcendentals=0
        ),
        name="curls",
    )(eps, marks, w, above, below)


def as_rows(x):
    return x.transpose(1, 2, 3, 0, 4).reshape(ROWS, V, 128)


def as_block(rows):
    return rows.reshape(3, NZ, NY, V, 128).transpose(3, 0, 1, 2, 4)


def per_device(current, search, previous, coefficients, material, inverse_permittivity):
    w, p, x = as_rows(search), as_rows(previous), as_rows(current)
    slab, blk = lax.axis_index("slab"), lax.axis_index("blk")
    place = jnp.stack([slab // 16, (slab // 2) % 8, slab % 2, blk // 2, blk % 2])
    mark_below = ring_shift(material[NZ - 1 :], "slab", 1)
    marks = jnp.concatenate([mark_below, material]).reshape((NZ + 1) * NY, 128)
    packed = pack(w, p, x)
    plane = gather_plane(coefficients)
    packed, plane = lax.optimization_barrier((packed, plane))
    cells = lax.all_to_all(packed, "blk", split_axis=0, concat_axis=0, tiled=True)
    groups = [[h * 16 + z * 2 + c for z in range(8)] for h in range(2) for c in range(2)]
    mine = lax.all_gather(plane, "slab", axis_index_groups=groups)
    other = move(mine, "slab", SLAB, (0, 0, 1))
    coef = assemble(place, mine, other)
    layers = w.reshape(3, NZ, NY, V, 128)
    low = layers[:2, 0].reshape(2 * NY, V, 128)
    high = layers[:, NZ - 1].reshape(3 * NY, V, 128)
    low, high = hold([low, high], [mine])
    above = ring_shift(low, "slab", -1)
    below = ring_shift(high, "slab", 1)
    applied, token = apply_curls(w, above, below, marks, inverse_permittivity.reshape(NMAT, 9))
    parts = rotate(cells, coef, token)
    back = lax.all_to_all(parts, "blk", split_axis=0, concat_axis=0, tiled=True)
    direction, rotated = unpack(back)
    return as_block(applied), as_block(rotated), as_block(direction)


def solution(mesh):
    block = P("blk", None, "slab", None, None)
    return jax.shard_map(
        per_device,
        mesh=mesh,
        in_specs=(block, block, block, P("slab", "blk"), P("slab", None, None), P()),
        out_specs=(block, block, block),
        check_vma=False,
    )
```

```python
import functools
import itertools

import jax
import jax.numpy as jnp
from jax import lax
from jax.experimental import pallas as pl
from jax.experimental.pallas import tpu as pltpu
from jax.sharding import PartitionSpec as P

M = 768
NMAT = 4
V = 96
NB = 8
ROWS = 81
SHARE = 10
LANES = 128 // NB
PART = SHARE * V
HALF = V // 2
SLAB = (2, 8, 2)
BLK = (4, 2)
ANY = pl.BlockSpec(memory_space=pl.ANY)
MIB = 1024 * 1024


def move(x, axis, sizes, steps):
    pairs = []
    for place in itertools.product(*[range(n) for n in sizes]):
        src = dst = 0
        for n, p, s in zip(sizes, place, steps):
            src = src * n + p
            dst = dst * n + (p + s) % n
        pairs.append((src, dst))
    return lax.ppermute(x, axis, pairs)


def ring_shift(x, axis, by):
    count = lax.axis_size(axis)
    return lax.ppermute(x, axis, [(i, (i + by) % count) for i in range(count)])


def gather_plane(tile):
    pieces = [tile]
    pieces.append(move(tile, "blk", BLK, (0, 1)))
    pieces.append(move(tile, "slab", SLAB, (1, 0, 0)))
    pieces.append(
        lax.ppermute(
            tile,
            ("slab", "blk"),
            [
                (s * NB + b, (s + 16) % 32 * NB + (b ^ 1))
                for s in range(32)
                for b in range(NB)
            ],
        )
    )
    t = jnp.stack(pieces)
    return jnp.stack([t] + [move(t, "blk", BLK, (-k, 0)) for k in (1, 2, 3)])


def assemble_kernel(place_ref, mine_ref, other_ref, out_ref):
    here, core = place_ref[0], place_ref[2]
    tiles = []
    for y_hi in range(2):
        k = (y_hi - here + 2) % 2
        for z in range(8):
            own = mine_ref[z, 0, k, 0].astype(jnp.float32)
            far = other_ref[z, 0, k, 0].astype(jnp.float32)
            tiles.append(jnp.where(core == 0, own, far))
            tiles.append(jnp.where(core == 0, far, own))
    out_ref[...] = jnp.concatenate(tiles, axis=0).T.astype(jnp.bfloat16)


def assemble(place, mine, other):
    def piece(b, at):
        return 0, (b // 2 - at[3] + 4) % 4, 0, (b % 2 - at[4] + 2) % 2, 0, 0

    mine, other = (t.reshape(8, 4, 2, 2, 72, 96) for t in (mine, other))
    pieces = pl.BlockSpec((8, 1, 2, 1, 72, 96), piece)
    return pl.pallas_call(
        assemble_kernel,
        out_shape=jax.ShapeDtypeStruct((M, 3 * M), jnp.bfloat16),
        grid_spec=pltpu.PrefetchScalarGridSpec(
            num_scalar_prefetch=1,
            grid=(NB,),
            in_specs=[pieces, pieces],
            out_specs=pl.BlockSpec((M // NB, 3 * M), lambda b, at: (b, 0)),
        ),
        compiler_params=pltpu.CompilerParams(vmem_limit_bytes=56 * MIB),
        cost_estimate=pl.CostEstimate(
            flops=10_000_000, bytes_accessed=8_000_000, transcendentals=0
        ),
        name="assemble",
    )(place, mine, other)


def lane_index(shape):
    return lax.broadcasted_iota(jnp.int32, shape, len(shape) - 1)


def rolled(x, by):
    by %= 128
    return x if by == 0 else pltpu.roll(x, by, x.ndim - 1)


def folded(row):
    lower = row[..., HALF:, :]
    shifted = rolled(lower.reshape(-1, 128), 64).reshape(lower.shape)
    return jnp.where(lane_index(lower.shape) < 64, row[..., :HALF, :], shifted)


def unfolded(half):
    shifted = rolled(half.reshape(-1, 128), 64).reshape(half.shape)
    return jnp.concatenate([half, shifted], axis=-2)


def pack_kernel(w_ref, p_ref, x_ref, out_ref, stage, tail, in_sems, tail_sems, out_sems):
    fields = (w_ref, p_ref, x_ref)
    last = [
        pltpu.make_async_copy(ref.at[pl.ds((ROWS - 1) * V, V)], tail.at[k], tail_sems.at[k])
        for k, ref in enumerate(fields)
    ]
    fetches = [
        [
            pltpu.make_async_copy(
                ref.at[pl.ds(PART * d, PART)],
                stage.at[d, pl.ds(PART * k, PART)],
                in_sems.at[d, k],
            )
            for k, ref in enumerate(fields)
        ]
        for d in range(NB)
    ]
    sends = [
        pltpu.make_async_copy(stage.at[d], out_ref.at[d], out_sems.at[d])
        for d in range(NB)
    ]
    for c in last:
        c.start()
    for group in fetches:
        for c in group:
            c.start()
    for c in last:
        c.wait()
    lane = lane_index((V, 128))
    w, p, x = (tail[k].astype(jnp.float32) for k in range(3))
    for d in range(NB):
        row = jnp.where(lane < 3 * LANES, rolled(x, LANES * (2 - d)), 0.0)
        row = jnp.where(lane < 2 * LANES, rolled(p, LANES * (1 - d)), row)
        row = jnp.where(lane < LANES, rolled(w, LANES * (0 - d)), row)
        stage[d, 3 * PART :] = folded(row).astype(jnp.bfloat16)
        for c in fetches[d]:
            c.wait()
        sends[d].start()
    for c in sends:
        c.wait()


def pack(w, p, x):
    shape = (NB, 3 * PART + HALF, 128)
    return pl.pallas_call(
        pack_kernel,
        out_shape=jax.ShapeDtypeStruct(shape, jnp.bfloat16),
        in_specs=[ANY] * 3,
        out_specs=ANY,
        scratch_shapes=[
            pltpu.VMEM(shape, jnp.bfloat16),
            pltpu.VMEM((3, V, 128), jnp.bfloat16),
            pltpu.SemaphoreType.DMA((NB, 3)),
            pltpu.SemaphoreType.DMA((3,)),
            pltpu.SemaphoreType.DMA((NB,)),
        ],
        compiler_params=pltpu.CompilerParams(vmem_limit_bytes=56 * MIB),
        cost_estimate=pl.CostEstimate(
            flops=2_000_000, bytes_accessed=12_000_000, transcendentals=0
        ),
        name="pack",
    )(*(t.reshape(ROWS * V, 128) for t in (w, p, x)))


def rotate_kernel(cells_ref, coef_ref, after_ref, out_ref, cells, out, in_sems, out_sems):
    del after_ref

    def fetch(k, i):
        rows = pl.ds(pl.multiple_of(PART * k + 2 * V * i, 2 * V), 2 * V)
        return pltpu.make_async_copy(
            cells_ref.at[:, rows], cells.at[:, rows], in_sems.at[k, i]
        )

    def put(k, i):
        rows = pl.ds(pl.multiple_of(PART * k + 2 * V * i, 2 * V), 2 * V)
        return pltpu.make_async_copy(
            out.at[:, rows], out_ref.at[:, rows], out_sems.at[k, i]
        )

    steps = SHARE // 2
    fetch_tail = pltpu.make_async_copy(
        cells_ref.at[:, pl.ds(3 * PART, HALF)],
        cells.at[:, pl.ds(3 * PART, HALF)],
        in_sems.at[0, steps],
    )
    put_tail = pltpu.make_async_copy(
        out.at[:, pl.ds(2 * PART, HALF)],
        out_ref.at[:, pl.ds(2 * PART, HALF)],
        out_sems.at[0, steps],
    )
    for i in range(steps):
        for k in range(3):
            fetch(k, i).start()
    fetch_tail.start()

    def product(w, p, x):
        wp = jnp.concatenate([w, p], axis=0)
        direction = jnp.dot(
            coef_ref[:, M:], wp, preferred_element_type=jnp.float32
        )
        rotated = direction + jnp.dot(
            coef_ref[:, :M], x, preferred_element_type=jnp.float32
        )
        return direction, rotated

    def row(k, i, j):
        return pl.ds(pl.multiple_of(PART * k + 2 * V * i + V * j, V), V)

    def step(i, carry):
        for k in range(3):
            fetch(k, i).wait()

        def row_pair(k):
            pair = [cells[:, row(k, i, j)].reshape(M, 128) for j in range(2)]
            return jnp.concatenate(pair, axis=1)

        results = product(row_pair(0), row_pair(1), row_pair(2))
        for k, result in enumerate(results):
            result = result.astype(jnp.bfloat16)
            for j in range(2):
                part = result[:, 128 * j : 128 * (j + 1)]
                out[:, row(k, i, j)] = part.reshape(NB, V, 128)
            put(k, i).start()
        return carry

    lax.fori_loop(0, steps, step, 0)
    fetch_tail.wait()
    wide = unfolded(cells[:, 3 * PART :].astype(jnp.float32)).reshape(M, 128)
    tail = wide.astype(jnp.bfloat16)
    shifted = [rolled(wide, -LANES * k).astype(jnp.bfloat16) for k in (1, 2)]
    direction, rotated = product(tail, *shifted)
    mixed = jnp.where(
        lane_index((M, 128)) < LANES, direction, rolled(rotated, LANES)
    )
    out[:, 2 * PART :] = folded(mixed.reshape(NB, V, 128)).astype(jnp.bfloat16)
    put_tail.start()
    for k in range(2):
        for i in range(steps):
            put(k, i).wait()
    put_tail.wait()


def rotate(cells, coef, after):
    return pl.pallas_call(
        rotate_kernel,
        out_shape=jax.ShapeDtypeStruct((NB, 2 * PART + HALF, 128), jnp.bfloat16),
        in_specs=[ANY, pl.BlockSpec(memory_space=pltpu.VMEM), ANY],
        out_specs=ANY,
        scratch_shapes=[
            pltpu.VMEM((NB, 3 * PART + HALF, 128), jnp.bfloat16),
            pltpu.VMEM((NB, 2 * PART + HALF, 128), jnp.bfloat16),
            pltpu.SemaphoreType.DMA((3, SHARE // 2 + 1)),
            pltpu.SemaphoreType.DMA((2, SHARE // 2 + 1)),
        ],
        compiler_params=pltpu.CompilerParams(vmem_limit_bytes=24 * MIB),
        cost_estimate=pl.CostEstimate(
            flops=6 * M * M * 128 * (SHARE + 1), bytes_accessed=14_000_000, transcendentals=0
        ),
        name="rotate",
    )(cells, coef, after)


def unpack_kernel(parts, d_ref, r_ref, last, out_sems, last_sems):
    copies = []
    for s in range(NB):
        for k, ref in enumerate((d_ref, r_ref)):
            copies.append(
                pltpu.make_async_copy(
                    parts.at[s, pl.ds(PART * k, PART)],
                    ref.at[pl.ds(PART * s, PART)],
                    out_sems.at[s, k],
                )
            )
            copies[-1].start()
    which = lane_index((V, 128)) // LANES
    direction = rotated = jnp.zeros((V, 128), jnp.float32)
    for s in range(NB):
        row = unfolded(parts[s, 2 * PART :].astype(jnp.float32))
        direction = jnp.where(which == s, rolled(row, LANES * s), direction)
        rotated = jnp.where(which == s, rolled(row, LANES * (s - 1)), rotated)
    last[0] = direction.astype(jnp.bfloat16)
    last[1] = rotated.astype(jnp.bfloat16)
    for k, ref in enumerate((d_ref, r_ref)):
        copies.append(pltpu.make_async_copy(last.at[k], ref.at[pl.ds((ROWS - 1) * V, V)], last_sems.at[k]))
        copies[-1].start()
    for c in copies:
        c.wait()


def unpack(parts):
    whole = jax.ShapeDtypeStruct((ROWS * V, 128), jnp.bfloat16)
    return pl.pallas_call(
        unpack_kernel,
        out_shape=(whole, whole),
        in_specs=[pl.BlockSpec(memory_space=pltpu.VMEM)],
        out_specs=(ANY, ANY),
        scratch_shapes=[
            pltpu.VMEM((2, V, 128), jnp.bfloat16),
            pltpu.SemaphoreType.DMA((NB, 2)),
            pltpu.SemaphoreType.DMA((2,)),
        ],
        compiler_params=pltpu.CompilerParams(vmem_limit_bytes=12 * MIB),
        name="unpack",
    )(parts)


def hold(arrays, until):
    count = len(arrays)

    def kernel(*refs):
        del refs

    return pl.pallas_call(
        kernel,
        out_shape=[jax.ShapeDtypeStruct(x.shape, x.dtype) for x in arrays],
        in_specs=[ANY] * (count + len(until)),
        out_specs=[ANY] * count,
        input_output_aliases={i: i for i in range(count)},
        name="hold",
    )(*arrays, *until)


NZ, NY = 3, 9
VB = 16


def curl_kernel(
    eps_ref, mat_ref, w_ref, above_ref, below_ref, out_ref, token_ref, tensor, electric
):
    token_ref[...] = jnp.zeros_like(token_ref)

    @pl.when(pl.program_id(0) == 0)
    def _():
        marks = mat_ref[...]
        for c in range(3):
            for d in range(3):
                value = jnp.full(marks.shape, eps_ref[0, c * 3 + d], jnp.float32)
                for m in range(1, NMAT):
                    value = jnp.where(marks == m, eps_ref[m, c * 3 + d], value)
                tensor[c * 3 + d] = 0.25 * value

    def field(c, z, y):
        y %= NY
        if z < 0:
            tile = below_ref[c * NY + y]
        elif z < NZ:
            tile = w_ref[(c * NZ + z) * NY + y]
        else:
            tile = above_ref[c * NY + y]
        return tile.astype(jnp.float32)

    for z in range(-1, NZ):
        for y in range(NY):
            hx, hy, hz = (field(c, z, y) for c in range(3))
            curl = (
                (field(2, z, y + 1) - hz) - (field(1, z + 1, y) - hy),
                (field(0, z + 1, y) - hx) - (rolled(hz, -1) - hz),
                (rolled(hy, -1) - hy) - (field(0, z, y + 1) - hx),
            )
            for c in range(3 if z >= 0 else 2):
                total = None
                for d in range(3):
                    weight = tensor[c * 3 + d, pl.ds((z + 1) * NY + y, 1)]
                    term = weight * curl[d]
                    total = term if total is None else total + term
                electric[c, (z + 1) * NY + y] = total
    for z in range(NZ):
        for y in range(NY):
            before = (y - 1) % NY
            here = (z + 1) * NY
            ex, ey, ez = (electric[c, here + y] for c in range(3))
            applied = (
                (ez - electric[2, here + before]) - (ey - electric[1, here + y - NY]),
                (ex - electric[0, here + y - NY]) - (ez - rolled(ez, 1)),
                (ey - rolled(ey, 1)) - (ex - electric[0, here + before]),
            )
            for c in range(3):
                out_ref[(c * NZ + z) * NY + y] = applied[c].astype(jnp.bfloat16)


def apply_curls(w, above, below, marks, eps):
    block = lambda rows: pl.BlockSpec((rows, VB, 128), lambda i: (0, i, 0))
    return pl.pallas_call(
        curl_kernel,
        out_shape=(
            jax.ShapeDtypeStruct((ROWS, V, 128), jnp.bfloat16),
            jax.ShapeDtypeStruct((8, 128), jnp.float32),
        ),
        grid=(V // VB,),
        in_specs=[
            pl.BlockSpec(memory_space=pltpu.SMEM),
            pl.BlockSpec(memory_space=pltpu.VMEM),
            block(ROWS),
            block(2 * NY),
            block(3 * NY),
        ],
        out_specs=(block(ROWS), pl.BlockSpec((8, 128), lambda i: (0, 0))),
        scratch_shapes=[
            pltpu.VMEM((9, (NZ + 1) * NY, 128), jnp.float32),
            pltpu.VMEM((3, (NZ + 1) * NY, VB, 128), jnp.float32),
        ],
        compiler_params=pltpu.CompilerParams(vmem_limit_bytes=56 * MIB),
        cost_estimate=pl.CostEstimate(
            flops=60_000_000, bytes_accessed=5_000_000, transcendentals=0
        ),
        name="curls",
    )(eps, marks, w, above, below)


def as_rows(x):
    return x.transpose(1, 2, 3, 0, 4).reshape(ROWS, V, 128)


def as_block(rows):
    return rows.reshape(3, NZ, NY, V, 128).transpose(3, 0, 1, 2, 4)


def per_device(current, search, previous, coefficients, material, inverse_permittivity):
    w, p, x = as_rows(search), as_rows(previous), as_rows(current)
    slab, blk = lax.axis_index("slab"), lax.axis_index("blk")
    place = jnp.stack([slab // 16, (slab // 2) % 8, slab % 2, blk // 2, blk % 2])
    mark_below = ring_shift(material[NZ - 1 :], "slab", 1)
    marks = jnp.concatenate([mark_below, material]).reshape((NZ + 1) * NY, 128)
    packed = pack(w, p, x)
    plane = gather_plane(coefficients)
    packed, plane = lax.optimization_barrier((packed, plane))
    cells = lax.all_to_all(packed, "blk", split_axis=0, concat_axis=0, tiled=True)
    groups = [[h * 16 + z * 2 + c for z in range(8)] for h in range(2) for c in range(2)]
    mine = lax.all_gather(plane, "slab", axis_index_groups=groups)
    other = move(mine, "slab", SLAB, (0, 0, 1))
    coef = assemble(place, mine, other)
    layers = w.reshape(3, NZ, NY, V, 128)
    low = layers[:2, 0].reshape(2 * NY, V, 128)
    high = layers[:, NZ - 1].reshape(3 * NY, V, 128)
    low, high = hold([low, high], [mine])
    above = ring_shift(low, "slab", -1)
    below = ring_shift(high, "slab", 1)
    applied, token = apply_curls(w, above, below, marks, inverse_permittivity.reshape(NMAT, 9))
    parts = rotate(cells, coef, token)
    back = lax.all_to_all(parts, "blk", split_axis=0, concat_axis=0, tiled=True)
    direction, rotated = unpack(back)
    return as_block(applied), as_block(rotated), as_block(direction)


def solution(mesh):
    block = P("blk", None, "slab", None, None)
    return jax.shard_map(
        per_device,
        mesh=mesh,
        in_specs=(block, block, block, P("slab", "blk"), P("slab", None, None), P()),
        out_specs=(block, block, block),
        check_vma=False,
    )
```

```python
import functools
import itertools

import jax
import jax.numpy as jnp
from jax import lax
from jax.experimental import pallas as pl
from jax.experimental.pallas import tpu as pltpu
from jax.sharding import PartitionSpec as P

M = 768
NMAT = 4
V = 96
NB = 8
ROWS = 81
SHARE = 10
LANES = 128 // NB
PART = SHARE * V
HALF = V // 2
SLAB = (2, 8, 2)
BLK = (4, 2)
ANY = pl.BlockSpec(memory_space=pl.ANY)
MIB = 1024 * 1024


def move(x, axis, sizes, steps):
    pairs = []
    for place in itertools.product(*[range(n) for n in sizes]):
        src = dst = 0
        for n, p, s in zip(sizes, place, steps):
            src = src * n + p
            dst = dst * n + (p + s) % n
        pairs.append((src, dst))
    return lax.ppermute(x, axis, pairs)


def ring_shift(x, axis, by):
    count = lax.axis_size(axis)
    return lax.ppermute(x, axis, [(i, (i + by) % count) for i in range(count)])


def gather_plane(tile):
    pieces = [tile]
    pieces.append(move(tile, "blk", BLK, (0, 1)))
    pieces.append(move(tile, "slab", SLAB, (1, 0, 0)))
    pieces.append(
        lax.ppermute(
            tile,
            ("slab", "blk"),
            [
                (s * NB + b, (s + 16) % 32 * NB + (b ^ 1))
                for s in range(32)
                for b in range(NB)
            ],
        )
    )
    t = jnp.stack(pieces)
    return jnp.stack([t] + [move(t, "blk", BLK, (-k, 0)) for k in (1, 2, 3)])


def assemble_kernel(place_ref, mine_ref, other_ref, out_ref):
    here, core = place_ref[0], place_ref[2]
    tiles = []
    for y_hi in range(2):
        k = (y_hi - here + 2) % 2
        for z in range(8):
            own = mine_ref[z, 0, k, 0].astype(jnp.float32)
            far = other_ref[z, 0, k, 0].astype(jnp.float32)
            tiles.append(jnp.where(core == 0, own, far))
            tiles.append(jnp.where(core == 0, far, own))
    out_ref[...] = jnp.concatenate(tiles, axis=0).T.astype(jnp.bfloat16)


def assemble(place, mine, other):
    def piece(b, at):
        return 0, (b // 2 - at[3] + 4) % 4, 0, (b % 2 - at[4] + 2) % 2, 0, 0

    mine, other = (t.reshape(8, 4, 2, 2, 72, 96) for t in (mine, other))
    pieces = pl.BlockSpec((8, 1, 2, 1, 72, 96), piece)
    return pl.pallas_call(
        assemble_kernel,
        out_shape=jax.ShapeDtypeStruct((M, 3 * M), jnp.bfloat16),
        grid_spec=pltpu.PrefetchScalarGridSpec(
            num_scalar_prefetch=1,
            grid=(NB,),
            in_specs=[pieces, pieces],
            out_specs=pl.BlockSpec((M // NB, 3 * M), lambda b, at: (b, 0)),
        ),
        compiler_params=pltpu.CompilerParams(vmem_limit_bytes=56 * MIB),
        cost_estimate=pl.CostEstimate(
            flops=10_000_000, bytes_accessed=8_000_000, transcendentals=0
        ),
        name="assemble",
    )(place, mine, other)


def from_below(x, z, core, y_lo):
    both = ("slab", "blk")
    straight, first, second = [], [], []
    for h, k, c, b in itertools.product(range(2), range(8), range(2), range(NB)):
        s = h * 16 + k * 2 + c
        if k == 7 and c == 1 and b % 2 == 1:
            target = ((1 - h) * 16) * NB + b
            first.append((s * NB + b, (h * 16) * NB + b - 1))
            second.append(((h * 16) * NB + b - 1, target))
        else:
            straight.append((s * NB + b, (s + 1) % 32 * NB + b))
    half_way = lax.ppermute(x, both, first)
    direct = lax.ppermute(x, both, straight)
    round_about = lax.ppermute(half_way, both, second)
    other_way = (z == 0) & (core == 0) & (y_lo == 1)
    return jnp.where(other_way, round_about, direct)


def lane_index(shape):
    return lax.broadcasted_iota(jnp.int32, shape, len(shape) - 1)


def rolled(x, by):
    by %= 128
    return x if by == 0 else pltpu.roll(x, by, x.ndim - 1)


def folded(row):
    lower = row[..., HALF:, :]
    shifted = rolled(lower.reshape(-1, 128), 64).reshape(lower.shape)
    return jnp.where(lane_index(lower.shape) < 64, row[..., :HALF, :], shifted)


def unfolded(half):
    shifted = rolled(half.reshape(-1, 128), 64).reshape(half.shape)
    return jnp.concatenate([half, shifted], axis=-2)


def pack_kernel(w_ref, p_ref, x_ref, out_ref, stage, tail, in_sems, tail_sems, out_sems):
    fields = (w_ref, p_ref, x_ref)
    last = [
        pltpu.make_async_copy(ref.at[pl.ds((ROWS - 1) * V, V)], tail.at[k], tail_sems.at[k])
        for k, ref in enumerate(fields)
    ]
    fetches = [
        [
            pltpu.make_async_copy(
                ref.at[pl.ds(PART * d, PART)],
                stage.at[d, pl.ds(PART * k, PART)],
                in_sems.at[d, k],
            )
            for k, ref in enumerate(fields)
        ]
        for d in range(NB)
    ]
    sends = [
        pltpu.make_async_copy(stage.at[d], out_ref.at[d], out_sems.at[d])
        for d in range(NB)
    ]
    for c in last:
        c.start()
    for group in fetches:
        for c in group:
            c.start()
    for c in last:
        c.wait()
    lane = lane_index((V, 128))
    w, p, x = (tail[k].astype(jnp.float32) for k in range(3))
    for d in range(NB):
        row = jnp.where(lane < 3 * LANES, rolled(x, LANES * (2 - d)), 0.0)
        row = jnp.where(lane < 2 * LANES, rolled(p, LANES * (1 - d)), row)
        row = jnp.where(lane < LANES, rolled(w, LANES * (0 - d)), row)
        stage[d, 3 * PART :] = folded(row).astype(jnp.bfloat16)
        for c in fetches[d]:
            c.wait()
        sends[d].start()
    for c in sends:
        c.wait()


def pack(w, p, x):
    shape = (NB, 3 * PART + HALF, 128)
    return pl.pallas_call(
        pack_kernel,
        out_shape=jax.ShapeDtypeStruct(shape, jnp.bfloat16),
        in_specs=[ANY] * 3,
        out_specs=ANY,
        scratch_shapes=[
            pltpu.VMEM(shape, jnp.bfloat16),
            pltpu.VMEM((3, V, 128), jnp.bfloat16),
            pltpu.SemaphoreType.DMA((NB, 3)),
            pltpu.SemaphoreType.DMA((3,)),
            pltpu.SemaphoreType.DMA((NB,)),
        ],
        compiler_params=pltpu.CompilerParams(vmem_limit_bytes=56 * MIB),
        cost_estimate=pl.CostEstimate(
            flops=2_000_000, bytes_accessed=12_000_000, transcendentals=0
        ),
        name="pack",
    )(*(t.reshape(ROWS * V, 128) for t in (w, p, x)))


def rotate_kernel(cells_ref, coef_ref, after_ref, out_ref, cells, out, in_sems, out_sems):
    del after_ref

    def fetch(k, i):
        rows = pl.ds(pl.multiple_of(PART * k + 2 * V * i, 2 * V), 2 * V)
        return pltpu.make_async_copy(
            cells_ref.at[:, rows], cells.at[:, rows], in_sems.at[k, i]
        )

    def put(k, i):
        rows = pl.ds(pl.multiple_of(PART * k + 2 * V * i, 2 * V), 2 * V)
        return pltpu.make_async_copy(
            out.at[:, rows], out_ref.at[:, rows], out_sems.at[k, i]
        )

    steps = SHARE // 2
    fetch_tail = pltpu.make_async_copy(
        cells_ref.at[:, pl.ds(3 * PART, HALF)],
        cells.at[:, pl.ds(3 * PART, HALF)],
        in_sems.at[0, steps],
    )
    put_tail = pltpu.make_async_copy(
        out.at[:, pl.ds(2 * PART, HALF)],
        out_ref.at[:, pl.ds(2 * PART, HALF)],
        out_sems.at[0, steps],
    )
    for i in range(steps):
        for k in range(3):
            fetch(k, i).start()
    fetch_tail.start()

    def product(w, p, x):
        wp = jnp.concatenate([w, p], axis=0)
        direction = jnp.dot(
            coef_ref[:, M:], wp, preferred_element_type=jnp.float32
        )
        rotated = direction + jnp.dot(
            coef_ref[:, :M], x, preferred_element_type=jnp.float32
        )
        return direction, rotated

    def row(k, i, j):
        return pl.ds(pl.multiple_of(PART * k + 2 * V * i + V * j, V), V)

    def step(i, carry):
        for k in range(3):
            fetch(k, i).wait()

        def row_pair(k):
            pair = [cells[:, row(k, i, j)].reshape(M, 128) for j in range(2)]
            return jnp.concatenate(pair, axis=1)

        results = product(row_pair(0), row_pair(1), row_pair(2))
        for k, result in enumerate(results):
            result = result.astype(jnp.bfloat16)
            for j in range(2):
                part = result[:, 128 * j : 128 * (j + 1)]
                out[:, row(k, i, j)] = part.reshape(NB, V, 128)
            put(k, i).start()
        return carry

    lax.fori_loop(0, steps, step, 0)
    fetch_tail.wait()
    wide = unfolded(cells[:, 3 * PART :].astype(jnp.float32)).reshape(M, 128)
    tail = wide.astype(jnp.bfloat16)
    shifted = [rolled(wide, -LANES * k).astype(jnp.bfloat16) for k in (1, 2)]
    direction, rotated = product(tail, *shifted)
    mixed = jnp.where(
        lane_index((M, 128)) < LANES, direction, rolled(rotated, LANES)
    )
    out[:, 2 * PART :] = folded(mixed.reshape(NB, V, 128)).astype(jnp.bfloat16)
    put_tail.start()
    for k in range(2):
        for i in range(steps):
            put(k, i).wait()
    put_tail.wait()


def rotate(cells, coef, after):
    return pl.pallas_call(
        rotate_kernel,
        out_shape=jax.ShapeDtypeStruct((NB, 2 * PART + HALF, 128), jnp.bfloat16),
        in_specs=[ANY, pl.BlockSpec(memory_space=pltpu.VMEM), ANY],
        out_specs=ANY,
        scratch_shapes=[
            pltpu.VMEM((NB, 3 * PART + HALF, 128), jnp.bfloat16),
            pltpu.VMEM((NB, 2 * PART + HALF, 128), jnp.bfloat16),
            pltpu.SemaphoreType.DMA((3, SHARE // 2 + 1)),
            pltpu.SemaphoreType.DMA((2, SHARE // 2 + 1)),
        ],
        compiler_params=pltpu.CompilerParams(vmem_limit_bytes=24 * MIB),
        cost_estimate=pl.CostEstimate(
            flops=6 * M * M * 128 * (SHARE + 1), bytes_accessed=14_000_000, transcendentals=0
        ),
        name="rotate",
    )(cells, coef, after)


def unpack_kernel(parts, d_ref, r_ref, last, out_sems, last_sems):
    copies = []
    for s in range(NB):
        for k, ref in enumerate((d_ref, r_ref)):
            copies.append(
                pltpu.make_async_copy(
                    parts.at[s, pl.ds(PART * k, PART)],
                    ref.at[pl.ds(PART * s, PART)],
                    out_sems.at[s, k],
                )
            )
            copies[-1].start()
    which = lane_index((V, 128)) // LANES
    direction = rotated = jnp.zeros((V, 128), jnp.float32)
    for s in range(NB):
        row = unfolded(parts[s, 2 * PART :].astype(jnp.float32))
        direction = jnp.where(which == s, rolled(row, LANES * s), direction)
        rotated = jnp.where(which == s, rolled(row, LANES * (s - 1)), rotated)
    last[0] = direction.astype(jnp.bfloat16)
    last[1] = rotated.astype(jnp.bfloat16)
    for k, ref in enumerate((d_ref, r_ref)):
        copies.append(pltpu.make_async_copy(last.at[k], ref.at[pl.ds((ROWS - 1) * V, V)], last_sems.at[k]))
        copies[-1].start()
    for c in copies:
        c.wait()


def unpack(parts):
    whole = jax.ShapeDtypeStruct((ROWS * V, 128), jnp.bfloat16)
    return pl.pallas_call(
        unpack_kernel,
        out_shape=(whole, whole),
        in_specs=[pl.BlockSpec(memory_space=pltpu.VMEM)],
        out_specs=(ANY, ANY),
        scratch_shapes=[
            pltpu.VMEM((2, V, 128), jnp.bfloat16),
            pltpu.SemaphoreType.DMA((NB, 2)),
            pltpu.SemaphoreType.DMA((2,)),
        ],
        compiler_params=pltpu.CompilerParams(vmem_limit_bytes=12 * MIB),
        name="unpack",
    )(parts)


def hold(arrays, until):
    count = len(arrays)

    def kernel(*refs):
        del refs

    return pl.pallas_call(
        kernel,
        out_shape=[jax.ShapeDtypeStruct(x.shape, x.dtype) for x in arrays],
        in_specs=[ANY] * (count + len(until)),
        out_specs=[ANY] * count,
        input_output_aliases={i: i for i in range(count)},
        name="hold",
    )(*arrays, *until)


NZ, NY = 3, 9
VB = 16


def curl_kernel(
    eps_ref, mat_ref, w_ref, above_ref, below_ref, out_ref, token_ref, tensor, electric
):
    token_ref[...] = jnp.zeros_like(token_ref)

    @pl.when(pl.program_id(0) == 0)
    def _():
        marks = mat_ref[...]
        for c in range(3):
            for d in range(3):
                value = jnp.full(marks.shape, eps_ref[0, c * 3 + d], jnp.float32)
                for m in range(1, NMAT):
                    value = jnp.where(marks == m, eps_ref[m, c * 3 + d], value)
                tensor[c * 3 + d] = 0.25 * value

    def field(c, z, y):
        y %= NY
        if z < 0:
            tile = below_ref[c * NY + y]
        elif z < NZ:
            tile = w_ref[(c * NZ + z) * NY + y]
        else:
            tile = above_ref[c * NY + y]
        return tile.astype(jnp.float32)

    for z in range(-1, NZ):
        for y in range(NY):
            hx, hy, hz = (field(c, z, y) for c in range(3))
            curl = (
                (field(2, z, y + 1) - hz) - (field(1, z + 1, y) - hy),
                (field(0, z + 1, y) - hx) - (rolled(hz, -1) - hz),
                (rolled(hy, -1) - hy) - (field(0, z, y + 1) - hx),
            )
            for c in range(3 if z >= 0 else 2):
                total = None
                for d in range(3):
                    weight = tensor[c * 3 + d, pl.ds((z + 1) * NY + y, 1)]
                    term = weight * curl[d]
                    total = term if total is None else total + term
                electric[c, (z + 1) * NY + y] = total
    for z in range(NZ):
        for y in range(NY):
            before = (y - 1) % NY
            here = (z + 1) * NY
            ex, ey, ez = (electric[c, here + y] for c in range(3))
            applied = (
                (ez - electric[2, here + before]) - (ey - electric[1, here + y - NY]),
                (ex - electric[0, here + y - NY]) - (ez - rolled(ez, 1)),
                (ey - rolled(ey, 1)) - (ex - electric[0, here + before]),
            )
            for c in range(3):
                out_ref[(c * NZ + z) * NY + y] = applied[c].astype(jnp.bfloat16)


def apply_curls(w, above, below, marks, eps):
    block = lambda rows: pl.BlockSpec((rows, VB, 128), lambda i: (0, i, 0))
    return pl.pallas_call(
        curl_kernel,
        out_shape=(
            jax.ShapeDtypeStruct((ROWS, V, 128), jnp.bfloat16),
            jax.ShapeDtypeStruct((8, 128), jnp.float32),
        ),
        grid=(V // VB,),
        in_specs=[
            pl.BlockSpec(memory_space=pltpu.SMEM),
            pl.BlockSpec(memory_space=pltpu.VMEM),
            block(ROWS),
            block(2 * NY),
            block(3 * NY),
        ],
        out_specs=(block(ROWS), pl.BlockSpec((8, 128), lambda i: (0, 0))),
        scratch_shapes=[
            pltpu.VMEM((9, (NZ + 1) * NY, 128), jnp.float32),
            pltpu.VMEM((3, (NZ + 1) * NY, VB, 128), jnp.float32),
        ],
        compiler_params=pltpu.CompilerParams(vmem_limit_bytes=56 * MIB),
        cost_estimate=pl.CostEstimate(
            flops=60_000_000, bytes_accessed=5_000_000, transcendentals=0
        ),
        name="curls",
    )(eps, marks, w, above, below)


def as_rows(x):
    return x.transpose(1, 2, 3, 0, 4).reshape(ROWS, V, 128)


def as_block(rows):
    return rows.reshape(3, NZ, NY, V, 128).transpose(3, 0, 1, 2, 4)


def per_device(current, search, previous, coefficients, material, inverse_permittivity):
    w, p, x = as_rows(search), as_rows(previous), as_rows(current)
    slab, blk = lax.axis_index("slab"), lax.axis_index("blk")
    place = jnp.stack([slab // 16, (slab // 2) % 8, slab % 2, blk // 2, blk % 2])
    mark_below = ring_shift(material[NZ - 1 :], "slab", 1)
    marks = jnp.concatenate([mark_below, material]).reshape((NZ + 1) * NY, 128)
    packed = pack(w, p, x)
    plane = gather_plane(coefficients)
    packed, plane = lax.optimization_barrier((packed, plane))
    cells = lax.all_to_all(packed, "blk", split_axis=0, concat_axis=0, tiled=True)
    groups = [[h * 16 + z * 2 + c for z in range(8)] for h in range(2) for c in range(2)]
    mine = lax.all_gather(plane, "slab", axis_index_groups=groups)
    other = move(mine, "slab", SLAB, (0, 0, 1))
    coef = assemble(place, mine, other)
    layers = w.reshape(3, NZ, NY, V, 128)
    low = layers[:2, 0].reshape(2 * NY, V, 128)
    high = layers[:, NZ - 1].reshape(3 * NY, V, 128)
    low, high = hold([low, high], [mine])
    above = ring_shift(low, "slab", -1)
    below = from_below(high, place[1], place[2], place[4])
    applied, token = apply_curls(w, above, below, marks, inverse_permittivity.reshape(NMAT, 9))
    parts = rotate(cells, coef, token)
    back = lax.all_to_all(parts, "blk", split_axis=0, concat_axis=0, tiled=True)
    direction, rotated = unpack(back)
    return as_block(applied), as_block(rotated), as_block(direction)


def solution(mesh):
    block = P("blk", None, "slab", None, None)
    return jax.shard_map(
        per_device,
        mesh=mesh,
        in_specs=(block, block, block, P("slab", "blk"), P("slab", None, None), P()),
        out_specs=(block, block, block),
        check_vma=False,
    )
```
